32 devices in a mesh: groups: 2 (over y), lat: 4 (over z), wid: 4 (over x, core).
Axes of the slice: x: 2, y: 2, z: 4, core: 2. Of those that a mesh axis runs over, the one named last changes fastest.
Arguments:
- errors: bfloat16 [2048, 8192], P(('groups', 'lat'), 'wid'), parts along dimension 0, may hold values from -8 to 8
- block_ids: int32 [2048, 4], P(('groups', 'lat')), parts along dimension 0, may hold values from 0 to 15, all different within a row; in each aligned block of 256 rows (0 to 255, 256 to 511, ...) at most 128 rows name the same one
- code_values: bfloat16 [2048, 4, 128], P(('groups', 'lat')), parts along dimension 0, may hold values from 0 to 2
- decoder: float32 [4096, 8192], P(('groups', 'lat'), 'wid'), parts along dimension 0, may hold values from -1 to 1
- first_moment: float32 [4096, 8192], P(('groups', 'lat'), 'wid'), parts along dimension 0, may hold values from -12 to 12
- second_moment: float32 [4096, 8192], P(('groups', 'lat'), 'wid'), parts along dimension 0, may hold values from 1 to 400
Outputs:
- new_decoder: float32 [4096, 8192], P(('groups', 'lat'), 'wid'), parts along dimension 0
- new_first: float32 [4096, 8192], P(('groups', 'lat'), 'wid'), parts along dimension 0
- new_second: float32 [4096, 8192], P(('groups', 'lat'), 'wid'), parts along dimension 0
The draws below stay inside these ranges and needn't reach their ends.
There are 2 independent parts, one for each index of `groups`. The reference program is written for one: setup_inputs(seed, part) draws one part's arguments, and reference() takes and returns one part's arrays. A program takes and returns all parts, laid end to end along the dimension named above; each array names one. Nothing has to cross between parts.
Inputs may be any that keep to these rules, and one draw needn't show every extreme that they name: `block_ids`: each row names 4 different blocks. In each aligned block of 256 rows no block is named by more than 128 rows, and some block is named by exactly 128.
All inputs are finite; a program needn't handle non-finite values.
Results may differ from the reference program's by a relative error of at most 0.0003.
Values may be sent and summed in bfloat16 or wider, within the bound.
No kernel may reach another device: no remote copies, remote signals or barrier semaphores. Data moves between devices by JAX's collectives and lax.ppermute only.
A program may use at most 128 MiB of HBM per device.

```python
import math
import jax
import jax.numpy as jnp
import numpy as np
from jax import lax

D = 8192
TOK_DEV = 256
KB = 4
BLOCK = 128
ADAM_STEP = 100
TOKENS = 1024
LATENTS = 2048
BLOCKS = 16
MOST = 128
N_LAT = 4


def scale_profile(key, count, span):
    return 10.0 ** jax.random.uniform(key, (count,), jnp.float32, 0.0, span)


def draw_errors(key, part):
    key = jax.random.fold_in(key, 11)
    streams = jax.random.split(key, 3)
    base = jax.random.normal(streams[0], (TOKENS, D), jnp.float32)
    rows = scale_profile(streams[1], TOKENS, 0.5) * 0.5
    columns = scale_profile(streams[2], D, 1.0) * 0.5
    values = base * rows[:, None] * columns[None, :]
    return jnp.clip(values, -8.0, 8.0).astype(jnp.bfloat16)


def draw_decoder(key, part):
    key = jax.random.fold_in(key, 23)
    streams = jax.random.split(key, 3)
    base = jax.random.normal(streams[0], (LATENTS, D), jnp.float32)
    rows = scale_profile(streams[1], LATENTS, 1.0) * 0.3
    columns = scale_profile(streams[2], D, 1.0) * 0.25
    values = base * rows[:, None] * columns[None, :] / jnp.sqrt(jnp.float32(D))
    return jnp.clip(values, -1.0, 1.0)


def block_levels(rng, extent, cuts, smallest, largest):
    loudness = 1.0
    for position, shards_of in cuts:
        heights = jax.random.uniform(jax.random.fold_in(jax.random.fold_in(rng, 6), position), (shards_of,), jnp.float32, smallest / len(cuts), largest / len(cuts))
        loudness = loudness * jnp.repeat(jnp.exp(heights), extent[position] // shards_of).reshape((-1,) + (1,) * (len(extent) - 1 - position))
    return loudness


def shared_out(stream_key, own, number, rows, number_of, top, most, skew):
    sequence = jax.random.permutation(stream_key, number_of)
    heavy_load, ordinary = load_shares(number_of, rows * top, most, skew, True), load_shares(number_of, rows * top, most, skew, False)
    places = jnp.arange(number_of)

    def named(sizes, turn):
        used = int((sizes > 0).sum())
        fixed = max(1, used // 4)
        shifted = fixed + (places - fixed + turn * (used - fixed)) % max(1, number_of - fixed)
        return jnp.zeros((number_of,), jnp.int32).at[sequence[jnp.where(places < fixed, places, shifted)]].set(jnp.asarray(sizes, jnp.int32))

    sizes = jnp.where(number % 4 == 0, named(heavy_load, number // 4), named(ordinary, number - number // 4 - 1))
    mixed = jax.random.permutation(jax.random.fold_in(own, 3), number_of)
    donor, sink = mixed[0:number_of // 2 * 2:2], mixed[1:number_of // 2 * 2:2]
    room = jnp.minimum(sizes[donor] - 1, most - sizes[sink]) // 2
    room = jnp.where((donor == sequence[0]) | (sink == sequence[0]) | (sizes[sink] == 0), 0, jnp.maximum(room, 0))
    shifted = jax.random.randint(jax.random.fold_in(own, 4), (number_of // 2,), 0, 1 << 20) % (room + 1)
    sizes = sizes.at[donor].add(-shifted).at[sink].add(shifted)
    items = jnp.searchsorted(jnp.cumsum(sizes), jnp.arange(rows * top), side="right").astype(jnp.int32)
    listing = items.reshape(top, rows).T
    listing = listing[jax.random.permutation(jax.random.fold_in(own, 1), rows)]
    turn = jax.random.randint(jax.random.fold_in(own, 2), (rows, 1), 0, top)
    return jnp.take_along_axis(listing, (jnp.arange(top)[None, :] + turn) % top, axis=1)


def load_shares(amount, total, reach, skew, full):
    portions = [(1 << 20) // math.isqrt(grade ** skew) + 1 for grade in range(1, amount + 1)]
    largest = reach if full else min(reach, max(-(-total // amount), total * portions[0] // sum(portions)))
    least = 1 if total - largest >= amount - 1 else 0
    counts, surplus = [largest] + [least] * (amount - 1), total - largest - least * (amount - 1)
    while surplus > 0:
        free = [i for i in range(1, amount) if counts[i] < largest] or [i for i in range(1, amount) if counts[i] < reach]
        pool, budget = sum([portions[i] for i in free]), surplus
        for i in free:
            extra = min(reach - counts[i], max(1, budget * portions[i] // pool), surplus)
            counts[i] = counts[i] + extra
            surplus = surplus - extra
    return np.array(counts)


def gaussian(key, extent, spread, reach, cuts=(), kind=jnp.bfloat16):
    array = spread * jax.random.normal(key, extent, jnp.float32)
    if cuts:
        array = array * block_levels(key, extent, cuts, -0.22, 0.18)
    return jnp.clip(array, -reach, reach).astype(kind)


def setup_inputs(seed: int = 0, part: int = 0) -> dict:
    arg_keys = jax.random.split(jax.random.key(seed), 7)
    part_splits = jax.random.split(jax.random.fold_in(arg_keys[6], part), 7)
    errors = draw_errors(jax.random.fold_in(jax.random.fold_in(arg_keys[6], part), 71), part)
    block_ids_keys = jax.random.split(jax.random.fold_in(part_splits[1], 1), TOKENS // TOK_DEV)
    block_ids_turns = jax.random.permutation(jax.random.fold_in(part_splits[1], 3), TOKENS // TOK_DEV)
    block_ids = jax.vmap(lambda own, number: shared_out(jax.random.fold_in(part_splits[1], 2), own, number, TOK_DEV, BLOCKS, KB, MOST, 2))(block_ids_keys, block_ids_turns).reshape((TOKENS, KB))
    code_values = jnp.clip(2.0 * jax.random.uniform(part_splits[2], (TOKENS, KB, BLOCK), jnp.float32) ** block_levels(part_splits[2], (TOKENS, KB, BLOCK), ((0, 4),), -0.2, 0.2), 0.0, 2.0).astype(jnp.bfloat16)
    decoder = draw_decoder(jax.random.fold_in(jax.random.fold_in(arg_keys[6], part), 71), part)
    first_moment = gaussian(part_splits[4], (LATENTS, D), 2.0, 12.0, ((0, 4), (1, 4)), jnp.float32)
    second_moment = jnp.clip(jnp.exp(math.log(400.0) - 5.9914645 * jax.random.uniform(part_splits[5], (LATENTS, D), jnp.float32) ** block_levels(part_splits[5], (LATENTS, D), ((0, 4), (1, 4)), -0.2, 0.2)), 1.0, 400.0)
    return {"errors": errors, "block_ids": block_ids, "code_values": code_values, "decoder": decoder, "first_moment": first_moment, "second_moment": second_moment}


beta_first = 0.9
beta_second = 0.999
learn_rate = 0.001
adam_epsilon = 1e-08
norm_epsilon = 1e-06

def reference(errors, block_ids, code_values, decoder, first_moment, second_moment):
    pairs = TOKENS * KB
    capacity = N_LAT * MOST
    flat_ids = block_ids.reshape(pairs).astype(jnp.int32)
    onehot = (flat_ids[:, None] == jnp.arange(BLOCKS, dtype=jnp.int32)[None, :]).astype(jnp.int32)
    before = lax.optimization_barrier(jnp.sum((jnp.cumsum(onehot, axis=0) - onehot) * onehot, axis=1)).astype(jnp.int32)
    target = flat_ids * capacity + before
    source = jnp.zeros((BLOCKS * capacity,), jnp.int32).at[target].set(jnp.arange(pairs, dtype=jnp.int32) + 1)
    source = source.reshape(BLOCKS, capacity)
    flat_codes = code_values.reshape(pairs, BLOCK)

    def one_block(owners):
        filled = owners > 0
        chosen = jnp.maximum(owners - 1, 0)
        rows = jnp.where(filled[:, None], errors[chosen // KB].astype(jnp.float32), jnp.float32(0.0))
        codes = jnp.where(filled[:, None], flat_codes[chosen].astype(jnp.float32), jnp.float32(0.0))
        return jnp.dot(codes.T, rows, precision=lax.Precision.HIGHEST, preferred_element_type=jnp.float32)
    gradient = lax.map(one_block, source).reshape(LATENTS, D)
    along = lax.optimization_barrier(jnp.sum(gradient * decoder, axis=1))
    squares = lax.optimization_barrier(jnp.sum(decoder * decoder, axis=1))
    projected = gradient - (along / (squares + norm_epsilon))[:, None] * decoder
    new_first = beta_first * first_moment + (1.0 - beta_first) * projected
    new_second = beta_second * second_moment + (1.0 - beta_second) * projected * projected
    moved = decoder - learn_rate * (new_first / (1.0 - beta_first ** ADAM_STEP)) / (jnp.sqrt(new_second / (1.0 - beta_second ** ADAM_STEP)) + adam_epsilon)
    length_sq = lax.optimization_barrier(jnp.sum(moved * moved, axis=1))
    new_decoder = moved / jnp.sqrt(length_sq + norm_epsilon)[:, None]
    return (new_decoder, new_first, new_second)
```

```python
import jax
import jax.numpy as jnp
from jax import lax
from jax.experimental import pallas as pl
from jax.experimental.pallas import tpu as pltpu
from jax.sharding import PartitionSpec as P

KB = 4
BLOCK = 128
ADAM_STEP = 100


beta_first = 0.9
beta_second = 0.999
learn_rate = 0.001
adam_epsilon = 1e-08
norm_epsilon = 1e-06

first_scale = 1.0 / (1.0 - beta_first**ADAM_STEP)
second_scale = 1.0 / (1.0 - beta_second**ADAM_STEP)

LANES = 128
PAIR = ((0, 1), (1, 0), (2, 3), (3, 2))
MIDDLE = ((1, 2), (2, 1))
OUTWARD = ((1, 0), (2, 3))
f32 = jnp.float32
VMEM_LIMIT = 48 * 1024 * 1024


def after(value, *earlier):
    return lax.optimization_barrier((value,) + earlier)[0]


def swap(value, axis, size, bit):
    return lax.ppermute(value, axis, [(i, i ^ bit) for i in range(size)])


def row_of(lanes):
    return jnp.sum(lanes.T, axis=0, keepdims=True)


def column_of(row):
    return jnp.broadcast_to(row, (LANES, row.shape[1])).T


def fold(block):
    total = block[:, :LANES]
    for left in range(LANES, block.shape[1], LANES):
        total = total + block[:, left : left + LANES]
    return total


def dense_kernel(place_ref, near_ref, far_ref, out_ref):
    tokens = near_ref.shape[2]
    blocks = out_ref.shape[0] // BLOCK
    first = place_ref[0] * blocks
    for source in range(4):
        packets = [ref[group * 4 + source] for ref in (near_ref, far_ref) for group in range(2)]
        values = [packet[:BLOCK].astype(f32) for packet in packets]
        names = [packet[BLOCK : BLOCK + 16].astype(f32)[:1] for packet in packets]
        for block in range(blocks):
            wanted = (first + block).astype(f32)
            total = jnp.zeros((BLOCK, tokens), f32)
            for value, name in zip(values, names):
                total = total + jnp.where(name == wanted, value, 0.0)
            out_ref[block * BLOCK : (block + 1) * BLOCK, source * tokens : (source + 1) * tokens] = (
                total.astype(jnp.bfloat16)
            )


def early_kernel(place_ref, codes_ref, own_ref, near0_ref, near1_ref, end20_ref, end21_ref, mid20_ref, mid21_ref,
                 end30_ref, mid30_ref, decoder_ref, grad_ref, along_ref, squares_ref, rows_ref):
    half = near0_ref.shape[0]
    at_end = place_ref[1] == 1
    rows_ref[0 : 2 * half] = own_ref[...]
    rows_ref[2 * half : 3 * half] = near0_ref[...]
    rows_ref[3 * half : 4 * half] = near1_ref[...]

    @pl.when(at_end)
    def _():
        rows_ref[4 * half : 5 * half] = end20_ref[...]
        rows_ref[5 * half : 6 * half] = end21_ref[...]
        rows_ref[6 * half : 7 * half] = end30_ref[...]

    @pl.when(jnp.logical_not(at_end))
    def _():
        rows_ref[4 * half : 5 * half] = mid20_ref[...]
        rows_ref[5 * half : 6 * half] = mid21_ref[...]
        rows_ref[6 * half : 7 * half] = mid30_ref[...]

    grad_ref[...] = jnp.dot(codes_ref[:, : 7 * half], rows_ref[...], preferred_element_type=f32)

    @pl.when(pl.program_id(0) == 0)
    def _():
        along_ref[...] = jnp.zeros_like(along_ref)
        squares_ref[...] = jnp.zeros_like(squares_ref)

    chunk = 64

    def step(index, carry):
        rows = pl.ds(pl.multiple_of(index * chunk, chunk), chunk)
        weights = decoder_ref[rows, :]
        along_ref[rows, :] += fold(grad_ref[rows, :] * weights)
        squares_ref[rows, :] += fold(weights * weights)
        return carry

    lax.fori_loop(0, grad_ref.shape[0] // chunk, step, 0)


def along_kernel(place_ref, codes_ref, end_ref, mid_ref, decoder_ref, along_ref, squares_ref, out_ref, last_ref, total_ref):
    step_now = pl.program_id(0)

    @pl.when(step_now == 0)
    def _():
        total_ref[...] = along_ref[...]

    rows_last = jnp.where(place_ref[1] == 1, end_ref[...], mid_ref[...])
    last_ref[...] = jnp.dot(codes_ref[...], rows_last, preferred_element_type=f32)
    chunk = 64

    def step(index, carry):
        rows = pl.ds(pl.multiple_of(index * chunk, chunk), chunk)
        total_ref[rows, :] += fold(last_ref[rows, :] * decoder_ref[rows, :])
        return carry

    lax.fori_loop(0, last_ref.shape[0] // chunk, step, 0)

    @pl.when(step_now == pl.num_programs(0) - 1)
    def _():
        out_ref[0:1, :] = row_of(total_ref[...])
        out_ref[1:2, :] = row_of(squares_ref[...])


def adam_kernel(place_ref, sum0_ref, sum1_ref, sum2_ref, sum3_ref, codes_ref, end_ref, mid_ref, grad_ref, decoder_ref,
                first_ref, second_ref, moved_ref, new_first_ref, new_second_ref, out_ref, last_ref, ratio_ref, total_ref):
    step_now = pl.program_id(0)

    @pl.when(step_now == 0)
    def _():
        sums = (sum0_ref[0:2, :] + sum1_ref[0:2, :]) + (sum2_ref[0:2, :] + sum3_ref[0:2, :])
        ratio_ref[...] = column_of(sums[0:1] / (sums[1:2] + norm_epsilon))
        total_ref[...] = jnp.zeros_like(total_ref)

    rows_last = jnp.where(place_ref[1] == 1, end_ref[...], mid_ref[...])
    last_ref[...] = jnp.dot(codes_ref[...], rows_last, preferred_element_type=f32)
    chunk = 32
    width = last_ref.shape[1]

    def step(index, carry):
        rows = pl.ds(pl.multiple_of(index * chunk, chunk), chunk)
        ratio = ratio_ref[rows, :]
        total = total_ref[rows, :]
        for left in range(0, width, LANES):
            columns = slice(left, left + LANES)
            weights = decoder_ref[rows, columns]
            projected = grad_ref[rows, columns] + last_ref[rows, columns] - ratio * weights
            new_first = beta_first * first_ref[rows, columns] + (1.0 - beta_first) * projected
            new_second = beta_second * second_ref[rows, columns] + ((1.0 - beta_second) * projected) * projected
            new_first_ref[rows, columns] = new_first
            new_second_ref[rows, columns] = new_second
            spread = jnp.sqrt(new_second * second_scale) + adam_epsilon
            moved = weights - (learn_rate * first_scale) * new_first / spread
            moved_ref[rows, columns] = moved
            total = total + moved * moved
        total_ref[rows, :] = total
        return carry

    lax.fori_loop(0, last_ref.shape[0] // chunk, step, 0)

    @pl.when(step_now == pl.num_programs(0) - 1)
    def _():
        out_ref[0:1, :] = row_of(total_ref[...])


def unit_kernel(sum0_ref, sum1_ref, sum2_ref, sum3_ref, moved_ref, out_ref, scale_ref):
    @pl.when(pl.program_id(0) == 0)
    def _():
        length = (sum0_ref[0:1, :] + sum1_ref[0:1, :]) + (sum2_ref[0:1, :] + sum3_ref[0:1, :])
        scale_ref[...] = column_of(1.0 / jnp.sqrt(length + norm_epsilon))

    chunk = 64

    def step(index, carry):
        rows = pl.ds(pl.multiple_of(index * chunk, chunk), chunk)
        scale = scale_ref[rows, :]
        for left in range(0, moved_ref.shape[1], LANES):
            out_ref[rows, left : left + LANES] = moved_ref[rows, left : left + LANES] * scale
        return carry

    lax.fori_loop(0, moved_ref.shape[0] // chunk, step, 0)


def whole(shape):
    return pl.BlockSpec(shape, lambda i: (0,) * len(shape))


def across(rows, width):
    return pl.BlockSpec((rows, width), lambda i: (0, i))


SCALARS = pl.BlockSpec(memory_space=pltpu.SMEM)


def shares(value):
    return [value] + [swap(value, "wid", 4, bit) for bit in (2, 3, 1)]


def chain_body(errors, block_ids, code_values, decoder, first_moment, second_moment):
    here = lax.axis_index("lat")
    wide = lax.axis_index("wid")
    at_end = (here == 0) | (here == 3)
    place = jnp.stack([here.astype(jnp.int32), at_end.astype(jnp.int32)])
    tokens, width = errors.shape
    half = tokens // 2
    latents = decoder.shape[0]

    halves = [errors[:half], errors[half:]]
    hop = lambda value, pairs: lax.ppermute(value, "lat", pairs)
    near, mid3, end2, mid2, end3 = [], [], [], [], []
    for part in halves:
        near.append(hop(part, PAIR))
        mid3.append(hop(part, MIDDLE))
    for i in range(2):
        end2.append(hop(after(mid3[i], near[i]), OUTWARD))
        mid2.append(hop(after(near[i], mid3[i]), MIDDLE))
    for i in range(2):
        end3.append(hop(after(mid2[i], end2[i]), OUTWARD))

    mine = lax.dynamic_index_in_dim(code_values, wide, 1, keepdims=False).T
    names = lax.dynamic_index_in_dim(block_ids, wide, 1, keepdims=False).astype(jnp.bfloat16)[None]
    packet = jnp.concatenate([mine, names, jnp.zeros((15, tokens), jnp.bfloat16)], axis=0)[None]
    packet = jnp.concatenate([packet, swap(packet, "lat", 4, 1)], axis=0)
    packet = jnp.concatenate([packet, swap(packet, "lat", 4, 2)], axis=0)
    packet = jnp.concatenate([packet, swap(packet, "wid", 4, 2)], axis=0)
    other = swap(packet, "wid", 4, 1)

    params = pltpu.CompilerParams(vmem_limit_bytes=VMEM_LIMIT)
    codes = pl.pallas_call(
        dense_kernel,
        out_shape=jax.ShapeDtypeStruct((latents, 4 * tokens), jnp.bfloat16),
        in_specs=[SCALARS] + [pl.BlockSpec(memory_space=pltpu.VMEM)] * 2,
        out_specs=pl.BlockSpec(memory_space=pltpu.VMEM),
        compiler_params=params,
    )(place, packet, other)

    block = 512
    lanes = jax.ShapeDtypeStruct((latents, LANES), f32)
    slab = jax.ShapeDtypeStruct((latents, width), f32)
    gradient, along, squares = pl.pallas_call(
        early_kernel,
        grid=(width // block,),
        out_shape=(slab, lanes, lanes),
        in_specs=[SCALARS, whole((latents, 4 * tokens)), across(tokens, block)]
        + [across(half, block)] * 8
        + [across(latents, block)],
        out_specs=(across(latents, block), whole((latents, LANES)), whole((latents, LANES))),
        scratch_shapes=[pltpu.VMEM((7 * half, block), jnp.bfloat16)],
        compiler_params=params,
    )(place, codes, errors, near[0], near[1], end2[0], end2[1], mid2[0], mid2[1], end3[0], mid3[0], decoder)

    last_codes = pl.BlockSpec((latents, half), lambda i: (0, 7))
    row_shape = jax.ShapeDtypeStruct((8, latents), f32)
    block = 512
    sums = pl.pallas_call(
        along_kernel,
        grid=(width // block,),
        out_shape=row_shape,
        in_specs=[SCALARS, last_codes, across(half, block), across(half, block), across(latents, block)]
        + [whole((latents, LANES))] * 2,
        out_specs=whole((8, latents)),
        scratch_shapes=[pltpu.VMEM((latents, block), f32), pltpu.VMEM((latents, LANES), f32)],
        compiler_params=params,
    )(place, codes, end3[1], mid3[1], decoder, along, squares)

    block = 256
    moved, new_first, new_second, lengths = pl.pallas_call(
        adam_kernel,
        grid=(width // block,),
        out_shape=(slab, slab, slab, row_shape),
        in_specs=[SCALARS] + [whole((8, latents))] * 4 + [last_codes, across(half, block), across(half, block)]
        + [across(latents, block)] * 4,
        out_specs=(across(latents, block),) * 3 + (whole((8, latents)),),
        scratch_shapes=[
            pltpu.VMEM((latents, block), f32),
            pltpu.VMEM((latents, LANES), f32),
            pltpu.VMEM((latents, LANES), f32),
        ],
        compiler_params=params,
    )(place, *shares(sums), codes, end3[1], mid3[1], gradient, decoder, first_moment, second_moment)

    block = 512
    new_decoder = pl.pallas_call(
        unit_kernel,
        grid=(width // block,),
        out_shape=slab,
        in_specs=[whole((8, latents))] * 4 + [across(latents, block)],
        out_specs=across(latents, block),
        scratch_shapes=[pltpu.VMEM((latents, LANES), f32)],
        compiler_params=params,
    )(*shares(lengths), moved)
    return (new_decoder, new_first, new_second)


def gather_body(errors, block_ids, code_values, decoder, first_moment, second_moment):
    here = lax.axis_index("lat")
    lat_dev = decoder.shape[0]
    blk_dev = lat_dev // BLOCK
    every_ids = lax.all_gather(block_ids, "lat", axis=0, tiled=True)
    owned = here * blk_dev + jnp.arange(blk_dev, dtype=jnp.int32)
    err_piece = lax.all_gather(errors, "lat", axis=0, tiled=True)
    code_piece = lax.all_gather(code_values, "lat", axis=0, tiled=True)
    count = err_piece.shape[0]
    dense = jnp.zeros((count, blk_dev, BLOCK), jnp.bfloat16)
    for position in range(KB):
        match = every_ids[:, position][:, None] == owned[None, :]
        dense = dense + jnp.where(
            match[:, :, None], code_piece[:, position][:, None, :], jnp.zeros((), jnp.bfloat16)
        )
    dense = dense.reshape(count, blk_dev * BLOCK)
    gradient = lax.dot_general(
        dense, err_piece, (((0,), (0,)), ((), ())), preferred_element_type=jnp.float32
    )
    along, row_squares = lax.psum(
        (jnp.sum(gradient * decoder, axis=1), jnp.sum(decoder * decoder, axis=1)), "wid"
    )
    projected = gradient - (along / (row_squares + norm_epsilon))[:, None] * decoder
    new_first = beta_first * first_moment + (1.0 - beta_first) * projected
    new_second = beta_second * second_moment + (1.0 - beta_second) * projected * projected
    moved = decoder - learn_rate * (new_first / (1.0 - beta_first**ADAM_STEP)) / (
        jnp.sqrt(new_second / (1.0 - beta_second**ADAM_STEP)) + adam_epsilon
    )
    length_sq = lax.psum(jnp.sum(moved * moved, axis=1), "wid")
    new_decoder = moved / jnp.sqrt(length_sq + norm_epsilon)[:, None]
    return (new_decoder, new_first, new_second)


def solution(mesh):
    chain = mesh.shape["lat"] == 4 and mesh.shape["wid"] == 4
    in_specs = (
        P(("groups", "lat"), "wid"),
        P(("groups", "lat"), None),
        P(("groups", "lat"), None, None),
        P(("groups", "lat"), "wid"),
        P(("groups", "lat"), "wid"),
        P(("groups", "lat"), "wid"),
    )
    out_specs = (
        P(("groups", "lat"), "wid"),
        P(("groups", "lat"), "wid"),
        P(("groups", "lat"), "wid"),
    )
    body = chain_body if chain else gather_body
    return jax.shard_map(body, mesh=mesh, in_specs=in_specs, out_specs=out_specs, check_vma=False)
```

```python
import jax
import jax.numpy as jnp
from jax import lax
from jax.experimental import pallas as pl
from jax.experimental.pallas import tpu as pltpu
from jax.sharding import PartitionSpec as P

KB = 4
BLOCK = 128
ADAM_STEP = 100


beta_first = 0.9
beta_second = 0.999
learn_rate = 0.001
adam_epsilon = 1e-08
norm_epsilon = 1e-06

first_scale = 1.0 / (1.0 - beta_first**ADAM_STEP)
second_scale = 1.0 / (1.0 - beta_second**ADAM_STEP)

LANES = 128
PAIR = ((0, 1), (1, 0), (2, 3), (3, 2))
MIDDLE = ((1, 2), (2, 1))
OUTWARD = ((1, 0), (2, 3))
f32 = jnp.float32


def after(value, *earlier):
    return lax.optimization_barrier((value,) + earlier)[0]


def swap(value, axis, size, bit):
    return lax.ppermute(value, axis, [(i, i ^ bit) for i in range(size)])


def row_of(lanes):
    return jnp.sum(lanes.T, axis=0, keepdims=True)


def column_of(row):
    return jnp.broadcast_to(row, (LANES, row.shape[1])).T


def fold(block):
    total = block[:, :LANES]
    for left in range(LANES, block.shape[1], LANES):
        total = total + block[:, left : left + LANES]
    return total


def dense_kernel(place_ref, *refs):
    *packet_refs, out_ref = refs
    count, _, width = packet_refs[0].shape
    tokens = width - LANES
    blocks = out_ref.shape[0] // BLOCK
    first = place_ref[0] * blocks
    for source in range(count):
        packets = [ref[source] for ref in packet_refs]
        values = [packet[:, :tokens].astype(f32) for packet in packets]
        names = [packet[:16, tokens:].astype(f32) for packet in packets]
        names = [jnp.concatenate([name[i : i + 1] for i in range(tokens // LANES)], axis=1) for name in names]
        for block in range(blocks):
            wanted = (first + block).astype(f32)
            total = jnp.zeros((BLOCK, tokens), f32)
            for value, name in zip(values, names):
                total = total + jnp.where(name == wanted, value, 0.0)
            out_ref[block * BLOCK : (block + 1) * BLOCK, source * tokens : (source + 1) * tokens] = (
                total.astype(jnp.bfloat16)
            )


def early_kernel(codes_ref, decoder_ref, *refs):
    *piece_refs, grad_ref, squares_ref, rows_ref, sems = refs
    width = grad_ref.shape[1]
    copies, top = [], 0
    for index, piece in enumerate(piece_refs):
        high = piece.shape[0]
        copies.append(
            pltpu.make_async_copy(
                piece.at[:, pl.ds(0, width)], rows_ref.at[pl.ds(top, high)], sems.at[index]
            )
        )
        copies[-1].start()
        top += high
    chunk = 8

    def step(index, carry):
        rows = pl.ds(pl.multiple_of(index * chunk, chunk), chunk)
        weights = decoder_ref[rows, :]
        squares_ref[rows, :] = fold(weights * weights)
        return carry

    lax.fori_loop(0, grad_ref.shape[0] // chunk, step, 0, unroll=2)
    for copy in copies:
        copy.wait()
    block = 512
    tokens = codes_ref.shape[1] // 4
    for left in range(0, width, block):
        columns = slice(left, left + block)
        grad_ref[:, columns] = jnp.dot(
            codes_ref[:, : 3 * tokens], rows_ref[: 3 * tokens, columns], preferred_element_type=f32
        ) + jnp.dot(codes_ref[:, 2 * tokens :], rows_ref[3 * tokens :, columns], preferred_element_type=f32)


def along_kernel(codes_ref, last0_ref, last1_ref, early_ref, decoder_ref, squares_ref, grad_ref, out_ref, total_ref):
    half = last0_ref.shape[0]
    block = 512
    for left in range(0, grad_ref.shape[1], block):
        columns = slice(left, left + block)
        rows = jnp.concatenate([last0_ref[:, columns], last1_ref[:, columns]], axis=0)
        grad_ref[:, columns] = early_ref[:, columns] + jnp.dot(codes_ref[...], rows, preferred_element_type=f32)
    chunk = 8

    def step(index, carry):
        rows = pl.ds(pl.multiple_of(index * chunk, chunk), chunk)
        total_ref[rows, :] = fold(grad_ref[rows, :] * decoder_ref[rows, :])
        return carry

    lax.fori_loop(0, grad_ref.shape[0] // chunk, step, 0, unroll=2)
    out_ref[0:1, :] = row_of(total_ref[...])
    out_ref[1:2, :] = row_of(squares_ref[...])


def adam_kernel(sum0_ref, sum1_ref, sum2_ref, sum3_ref, grad_ref, decoder_ref, first_ref, second_ref,
                moved_ref, new_first_ref, new_second_ref, out_ref, ratio_ref, total_ref, first_buf, second_buf, sems):
    sums = (sum0_ref[0:2, :] + sum1_ref[0:2, :]) + (sum2_ref[0:2, :] + sum3_ref[0:2, :])
    ratio_ref[...] = column_of(sums[0:1] / (sums[1:2] + norm_epsilon))
    latents, width = grad_ref.shape
    part, chunk = 64, 16

    def copies(index):
        rows = pl.ds(index * part, part)
        return (
            pltpu.make_async_copy(first_buf.at[rows], new_first_ref.at[rows], sems.at[0, index]),
            pltpu.make_async_copy(second_buf.at[rows], new_second_ref.at[rows], sems.at[1, index]),
        )

    for index in range(latents // part):

        def step(inner, carry):
            rows = pl.ds(pl.multiple_of(index * part + inner * chunk, chunk), chunk)
            ratio = ratio_ref[rows, :]
            total = jnp.zeros((chunk, LANES), f32)
            for left in range(0, width, LANES):
                columns = slice(left, left + LANES)
                weights = decoder_ref[rows, columns]
                projected = grad_ref[rows, columns] - ratio * weights
                new_first = beta_first * first_ref[rows, columns] + (1.0 - beta_first) * projected
                new_second = beta_second * second_ref[rows, columns] + ((1.0 - beta_second) * projected) * projected
                first_buf[rows, columns] = new_first
                second_buf[rows, columns] = new_second
                unbiased = new_second * second_scale
                spread = unbiased * lax.rsqrt(unbiased) + adam_epsilon
                moved = weights - (learn_rate * first_scale) * new_first / spread
                moved_ref[rows, columns] = moved
                total = total + moved * moved
            total_ref[rows, :] = total
            return carry

        lax.fori_loop(0, part // chunk, step, 0)
        for copy in copies(index):
            copy.start()
    out_ref[0:1, :] = row_of(total_ref[...])
    for index in range(latents // part):
        for copy in copies(index):
            copy.wait()


def unit_kernel(sum0_ref, sum1_ref, sum2_ref, sum3_ref, moved_ref, out_ref, buf, sems):
    length = (sum0_ref[0:1, :] + sum1_ref[0:1, :]) + (sum2_ref[0:1, :] + sum3_ref[0:1, :])
    scale = column_of(1.0 / jnp.sqrt(length + norm_epsilon))
    latents, width = moved_ref.shape
    part = 32

    def copy(index):
        rows = pl.ds(index * part, part)
        return pltpu.make_async_copy(buf.at[rows], out_ref.at[rows], sems.at[index])

    for index in range(latents // part):
        rows = slice(index * part, (index + 1) * part)
        for left in range(0, width, LANES):
            buf[rows, left : left + LANES] = moved_ref[rows, left : left + LANES] * scale[rows]
        copy(index).start()
    for index in range(latents // part):
        copy(index).wait()


SCALARS = pl.BlockSpec(memory_space=pltpu.SMEM)
ONCHIP = pl.BlockSpec(memory_space=pltpu.VMEM)
OUTSIDE = pl.BlockSpec(memory_space=pl.ANY)


def resident(value):
    return pltpu.with_memory_space_constraint(value, pltpu.VMEM)


def outside(value):
    return pltpu.with_memory_space_constraint(value, pltpu.HBM)


def limit(mib):
    return pltpu.CompilerParams(vmem_limit_bytes=mib * 1024 * 1024)


def shares(value):
    return [value] + [swap(value, "wid", 4, bit) for bit in (2, 3, 1)]


def chain_body(errors, block_ids, code_values, decoder, first_moment, second_moment):
    here = lax.axis_index("lat")
    wide = lax.axis_index("wid")
    place = here.astype(jnp.int32)[None]
    tokens, width = errors.shape
    half = tokens // 2
    latents = decoder.shape[0]

    mine = lax.dynamic_index_in_dim(code_values, wide, 1, keepdims=False).T
    names = lax.dynamic_index_in_dim(block_ids, wide, 1, keepdims=False).astype(jnp.bfloat16)
    names = names.reshape(tokens // LANES, LANES)
    names = jnp.concatenate([names, jnp.zeros((half - names.shape[0], LANES), jnp.bfloat16)], axis=0)
    packet = jnp.concatenate([mine, names], axis=1)

    hop = lambda value, pairs: lax.ppermute(value, "lat", pairs)
    near, mid3, end2, mid2, end3 = [], [], [], [], []
    for part in (jnp.concatenate([errors[:half], packet], axis=1), lax.optimization_barrier(errors)[half:]):
        near.append(hop(part, PAIR))
        mid3.append(hop(part, MIDDLE))
    for i in range(2):
        end2.append(hop(after(mid3[i], near[i]), OUTWARD))
        mid2.append(hop(after(near[i], mid3[i]), MIDDLE))
    for i in range(2):
        end3.append(hop(after(mid2[i], end2[i]), OUTWARD))

    packets = jnp.stack([packet] + [part[:, width:] for part in (near[0], end2[0] + mid2[0], mid3[0])])
    late = end3[0][:, width:][None]

    def dense(count, *arrays):
        return pl.pallas_call(
            dense_kernel,
            out_shape=jax.ShapeDtypeStruct((latents, count * tokens), jnp.bfloat16),
            in_specs=[SCALARS] + [ONCHIP] * 4,
            out_specs=ONCHIP,
            compiler_params=limit(8),
        )(place, *arrays)

    codes = dense(4, *shares(packets))
    late_codes = dense(1, *shares(late))

    lanes = jax.ShapeDtypeStruct((latents, LANES), f32)
    slab = jax.ShapeDtypeStruct((latents, width), f32)
    kept_slab = pltpu.VMEM((latents, width), f32)
    row_shape = jax.ShapeDtypeStruct((8, latents), f32)
    kept_decoder = resident(decoder)
    early, squares = pl.pallas_call(
        early_kernel,
        out_shape=(kept_slab, lanes),
        in_specs=[ONCHIP] * 2 + [OUTSIDE] * 9,
        out_specs=(ONCHIP,) * 2,
        scratch_shapes=[pltpu.VMEM((5 * tokens, width), jnp.bfloat16), pltpu.SemaphoreType.DMA((9,))],
        compiler_params=limit(10),
        cost_estimate=pl.CostEstimate(flops=20 * latents * tokens * width, bytes_accessed=16 * latents * width, transcendentals=0),
    )(codes, kept_decoder, *map(outside, (errors, *near, *end2, *mid2, *mid3)))
    gradient, sums = pl.pallas_call(
        along_kernel,
        out_shape=(kept_slab, row_shape),
        in_specs=[ONCHIP] * 6,
        out_specs=(ONCHIP,) * 2,
        scratch_shapes=[pltpu.VMEM((latents, LANES), f32)],
        input_output_aliases={3: 0},
        compiler_params=limit(8),
    )(late_codes, resident(end3[0]), resident(end3[1]), resident(early), kept_decoder, squares)

    moved, new_first, new_second, lengths = pl.pallas_call(
        adam_kernel,
        out_shape=(kept_slab, slab, slab, row_shape),
        in_specs=[ONCHIP] * 8,
        out_specs=(ONCHIP, OUTSIDE, OUTSIDE, ONCHIP),
        scratch_shapes=[pltpu.VMEM((latents, LANES), f32)] * 2
        + [pltpu.VMEM((latents, width), f32)] * 2
        + [pltpu.SemaphoreType.DMA((2, latents // 64))],
        compiler_params=limit(12),
    )(*shares(sums), resident(gradient), kept_decoder, resident(first_moment), resident(second_moment))

    new_decoder = pl.pallas_call(
        unit_kernel,
        out_shape=slab,
        in_specs=[ONCHIP] * 5,
        out_specs=OUTSIDE,
        scratch_shapes=[pltpu.VMEM((latents, width), f32), pltpu.SemaphoreType.DMA((latents // 32,))],
        compiler_params=limit(8),
    )(*shares(lengths), resident(moved))
    return (new_decoder, new_first, new_second)


def gather_body(errors, block_ids, code_values, decoder, first_moment, second_moment):
    here = lax.axis_index("lat")
    lat_dev = decoder.shape[0]
    blk_dev = lat_dev // BLOCK
    every_ids = lax.all_gather(block_ids, "lat", axis=0, tiled=True)
    owned = here * blk_dev + jnp.arange(blk_dev, dtype=jnp.int32)
    err_piece = lax.all_gather(errors, "lat", axis=0, tiled=True)
    code_piece = lax.all_gather(code_values, "lat", axis=0, tiled=True)
    count = err_piece.shape[0]
    dense = jnp.zeros((count, blk_dev, BLOCK), jnp.bfloat16)
    for position in range(KB):
        match = every_ids[:, position][:, None] == owned[None, :]
        dense = dense + jnp.where(
            match[:, :, None], code_piece[:, position][:, None, :], jnp.zeros((), jnp.bfloat16)
        )
    dense = dense.reshape(count, blk_dev * BLOCK)
    gradient = lax.dot_general(
        dense, err_piece, (((0,), (0,)), ((), ())), preferred_element_type=jnp.float32
    )
    along, row_squares = lax.psum(
        (jnp.sum(gradient * decoder, axis=1), jnp.sum(decoder * decoder, axis=1)), "wid"
    )
    projected = gradient - (along / (row_squares + norm_epsilon))[:, None] * decoder
    new_first = beta_first * first_moment + (1.0 - beta_first) * projected
    new_second = beta_second * second_moment + (1.0 - beta_second) * projected * projected
    moved = decoder - learn_rate * (new_first / (1.0 - beta_first**ADAM_STEP)) / (
        jnp.sqrt(new_second / (1.0 - beta_second**ADAM_STEP)) + adam_epsilon
    )
    length_sq = lax.psum(jnp.sum(moved * moved, axis=1), "wid")
    new_decoder = moved / jnp.sqrt(length_sq + norm_epsilon)[:, None]
    return (new_decoder, new_first, new_second)


def solution(mesh):
    chain = mesh.shape["lat"] == 4 and mesh.shape["wid"] == 4
    in_specs = (
        P(("groups", "lat"), "wid"),
        P(("groups", "lat"), None),
        P(("groups", "lat"), None, None),
        P(("groups", "lat"), "wid"),
        P(("groups", "lat"), "wid"),
        P(("groups", "lat"), "wid"),
    )
    out_specs = (
        P(("groups", "lat"), "wid"),
        P(("groups", "lat"), "wid"),
        P(("groups", "lat"), "wid"),
    )
    body = chain_body if chain else gather_body
    return jax.shard_map(body, mesh=mesh, in_specs=in_specs, out_specs=out_specs, check_vma=False)
```

```python
import jax
import jax.numpy as jnp
from jax import lax
from jax.experimental import pallas as pl
from jax.experimental.pallas import tpu as pltpu
from jax.sharding import PartitionSpec as P

KB = 4
BLOCK = 128
ADAM_STEP = 100


beta_first = 0.9
beta_second = 0.999
learn_rate = 0.001
adam_epsilon = 1e-08
norm_epsilon = 1e-06

first_scale = 1.0 / (1.0 - beta_first**ADAM_STEP)
second_scale = 1.0 / (1.0 - beta_second**ADAM_STEP)

LANES = 128
PAIR = ((0, 1), (1, 0), (2, 3), (3, 2))
MIDDLE = ((1, 2), (2, 1))
OUTWARD = ((1, 0), (2, 3))
f32 = jnp.float32


def after(value, *earlier):
    return lax.optimization_barrier((value,) + earlier)[0]


def swap(value, axis, size, bit):
    return lax.ppermute(value, axis, [(i, i ^ bit) for i in range(size)])


def row_of(lanes):
    return jnp.sum(lanes.T, axis=0, keepdims=True)


def column_of(row):
    return jnp.broadcast_to(row, (LANES, row.shape[1])).T


def fold(block):
    total = block[:, :LANES]
    for left in range(LANES, block.shape[1], LANES):
        total = total + block[:, left : left + LANES]
    return total


def dense_kernel(place_ref, *refs):
    *packet_refs, out_ref = refs
    count, _, width = packet_refs[0].shape
    tokens = width - LANES
    blocks = out_ref.shape[0] // BLOCK
    first = place_ref[0] * blocks
    for source in range(count):
        packets = [ref[source] for ref in packet_refs]
        values = [packet[:, :tokens].astype(f32) for packet in packets]
        names = [packet[:16, tokens:].astype(f32) for packet in packets]
        names = [jnp.concatenate([name[i : i + 1] for i in range(tokens // LANES)], axis=1) for name in names]
        for block in range(blocks):
            wanted = (first + block).astype(f32)
            total = jnp.zeros((BLOCK, tokens), f32)
            for value, name in zip(values, names):
                total = total + jnp.where(name == wanted, value, 0.0)
            out_ref[block * BLOCK : (block + 1) * BLOCK, source * tokens : (source + 1) * tokens] = (
                total.astype(jnp.bfloat16)
            )


def squares_kernel(decoder_ref, out_ref):
    chunk = 8

    def step(index, carry):
        rows = pl.ds(pl.multiple_of(index * chunk, chunk), chunk)
        weights = decoder_ref[rows, :]
        out_ref[rows, :] = fold(weights * weights)
        return carry

    lax.fori_loop(0, out_ref.shape[0] // chunk, step, 0, unroll=2)


def early_kernel(codes_ref, *refs):
    *piece_refs, grad_ref, rows_ref, sems = refs
    width = grad_ref.shape[1]
    copies, top = [], 0
    for index, piece in enumerate(piece_refs):
        high = piece.shape[0]
        copies.append(
            pltpu.make_async_copy(
                piece.at[:, pl.ds(0, width)], rows_ref.at[pl.ds(top, high)], sems.at[index]
            )
        )
        copies[-1].start()
        top += high
    for copy in copies:
        copy.wait()
    block = 512
    tokens = codes_ref.shape[1] // 4
    for left in range(0, width, block):
        columns = slice(left, left + block)
        grad_ref[:, columns] = jnp.dot(
            codes_ref[:, : 3 * tokens], rows_ref[: 3 * tokens, columns], preferred_element_type=f32
        ) + jnp.dot(codes_ref[:, 2 * tokens :], rows_ref[3 * tokens :, columns], preferred_element_type=f32)


def along_kernel(codes_ref, last0_ref, last1_ref, early_ref, decoder_ref, squares_ref, grad_ref, out_ref, total_ref):
    half = last0_ref.shape[0]
    block = 512
    for left in range(0, grad_ref.shape[1], block):
        columns = slice(left, left + block)
        rows = jnp.concatenate([last0_ref[:, columns], last1_ref[:, columns]], axis=0)
        grad_ref[:, columns] = early_ref[:, columns] + jnp.dot(codes_ref[...], rows, preferred_element_type=f32)
    chunk = 8

    def step(index, carry):
        rows = pl.ds(pl.multiple_of(index * chunk, chunk), chunk)
        total_ref[rows, :] = fold(grad_ref[rows, :] * decoder_ref[rows, :])
        return carry

    lax.fori_loop(0, grad_ref.shape[0] // chunk, step, 0, unroll=2)
    out_ref[0:1, :] = row_of(total_ref[...])
    out_ref[1:2, :] = row_of(squares_ref[...])


def ratio_of(sum0_ref, sum1_ref, sum2_ref, sum3_ref):
    sums = (sum0_ref[0:2, :] + sum1_ref[0:2, :]) + (sum2_ref[0:2, :] + sum3_ref[0:2, :])
    return column_of(sums[0:1] / (sums[1:2] + norm_epsilon))


def second_of(projected, second):
    return beta_second * second + ((1.0 - beta_second) * projected) * projected


PART = 64


def rows_out(buf, target, sems):
    parts = [pl.ds(index * PART, PART) for index in range(buf.shape[0] // PART)]
    return [pltpu.make_async_copy(buf.at[rows], target.at[rows], sems.at[i]) for i, rows in enumerate(parts)]


def move_kernel(sum0_ref, sum1_ref, sum2_ref, sum3_ref, grad_ref, decoder_ref, first_ref, second_ref,
                moved_ref, ratio_ref, out_ref, new_first_ref, total_ref, first_buf, sems):
    ratio_ref[...] = ratio_of(sum0_ref, sum1_ref, sum2_ref, sum3_ref)
    width = grad_ref.shape[1]
    chunk = 8
    copies = rows_out(first_buf, new_first_ref, sems)
    for index, copy in enumerate(copies):

        def step(inner, carry):
            rows = pl.ds(pl.multiple_of(index * PART + inner * chunk, chunk), chunk)
            ratio = ratio_ref[rows, :]
            total = jnp.zeros((chunk, LANES), f32)
            for left in range(0, width, LANES):
                columns = slice(left, left + LANES)
                weights = decoder_ref[rows, columns]
                projected = grad_ref[rows, columns] - ratio * weights
                new_first = beta_first * first_ref[rows, columns] + (1.0 - beta_first) * projected
                first_buf[rows, columns] = new_first
                new_second = second_of(projected, second_ref[rows, columns])
                unbiased = new_second * second_scale
                spread = unbiased * lax.rsqrt(unbiased) + adam_epsilon
                moved = weights - (learn_rate * first_scale) * new_first / spread
                moved_ref[rows, columns] = moved
                total = total + moved * moved
            total_ref[rows, :] = total
            return carry

        lax.fori_loop(0, PART // chunk, step, 0, unroll=PART // chunk)
        copy.start()
    out_ref[0:1, :] = row_of(total_ref[...])
    for copy in copies:
        copy.wait()


def second_kernel(ratio_ref, grad_ref, decoder_ref, second_ref, new_second_ref, second_buf, sems):
    width = grad_ref.shape[1]
    chunk = 8
    copies = rows_out(second_buf, new_second_ref, sems)
    for index, copy in enumerate(copies):

        def step(inner, carry):
            rows = pl.ds(pl.multiple_of(index * PART + inner * chunk, chunk), chunk)
            ratio = ratio_ref[rows, :]
            for left in range(0, width, LANES):
                columns = slice(left, left + LANES)
                projected = grad_ref[rows, columns] - ratio * decoder_ref[rows, columns]
                second_buf[rows, columns] = second_of(projected, second_ref[rows, columns])
            return carry

        lax.fori_loop(0, PART // chunk, step, 0, unroll=4)
        copy.start()
    for copy in copies:
        copy.wait()


def unit_kernel(sum0_ref, sum1_ref, sum2_ref, sum3_ref, moved_ref, out_ref, buf, sems):
    length = (sum0_ref[0:1, :] + sum1_ref[0:1, :]) + (sum2_ref[0:1, :] + sum3_ref[0:1, :])
    scale = column_of(1.0 / jnp.sqrt(length + norm_epsilon))
    width = moved_ref.shape[1]
    copies = rows_out(buf, out_ref, sems)
    for index, copy in enumerate(copies):
        rows = slice(index * PART, (index + 1) * PART)
        for left in range(0, width, LANES):
            buf[rows, left : left + LANES] = moved_ref[rows, left : left + LANES] * scale[rows]
        copy.start()
    for copy in copies:
        copy.wait()


SCALARS = pl.BlockSpec(memory_space=pltpu.SMEM)
ONCHIP = pl.BlockSpec(memory_space=pltpu.VMEM)
OUTSIDE = pl.BlockSpec(memory_space=pl.ANY)


def resident(value):
    return pltpu.with_memory_space_constraint(value, pltpu.VMEM)


def outside(value):
    return pltpu.with_memory_space_constraint(value, pltpu.HBM)


def limit(mib):
    return pltpu.CompilerParams(vmem_limit_bytes=mib * 1024 * 1024)


def shares(value):
    return [value] + [swap(value, "wid", 4, bit) for bit in (2, 3, 1)]


def chain_body(errors, block_ids, code_values, decoder, first_moment, second_moment):
    here = lax.axis_index("lat")
    wide = lax.axis_index("wid")
    place = here.astype(jnp.int32)[None]
    tokens, width = errors.shape
    half = tokens // 2
    latents = decoder.shape[0]

    mine = lax.dynamic_index_in_dim(code_values, wide, 1, keepdims=False).T
    names = lax.dynamic_index_in_dim(block_ids, wide, 1, keepdims=False).astype(jnp.bfloat16)
    names = names.reshape(tokens // LANES, LANES)
    names = jnp.concatenate([names, jnp.zeros((half - names.shape[0], LANES), jnp.bfloat16)], axis=0)
    packet = jnp.concatenate([mine, names], axis=1)

    hop = lambda value, pairs: lax.ppermute(value, "lat", pairs)
    beside = lambda rows, codes: jnp.concatenate([rows, codes], axis=1)
    near = hop(errors, PAIR)
    near_packet = hop(packet, PAIR)
    mid3 = [hop(beside(errors[:half], packet), MIDDLE), hop(errors[half:], MIDDLE)]
    end2 = [hop(part, OUTWARD) for part in mid3]
    mid2 = [
        hop(beside(after(near, mid3[0])[:half], near_packet), MIDDLE),
        hop(after(near, mid3[1])[half:], MIDDLE),
    ]
    end3 = [hop(after(mid2[i], end2[i]), OUTWARD) for i in range(2)]

    packets = jnp.stack([packet, near_packet, (end2[0] + mid2[0])[:, width:], mid3[0][:, width:]])
    late = end3[0][:, width:][None]

    def dense(count, *arrays):
        return pl.pallas_call(
            dense_kernel,
            out_shape=jax.ShapeDtypeStruct((latents, count * tokens), jnp.bfloat16),
            in_specs=[SCALARS] + [ONCHIP] * 4,
            out_specs=ONCHIP,
            compiler_params=limit(8),
        )(place, *arrays)

    codes = dense(4, *shares(packets))
    late_codes = dense(1, *shares(late))

    lanes = jax.ShapeDtypeStruct((latents, LANES), f32)
    slab = jax.ShapeDtypeStruct((latents, width), f32)
    kept_slab = pltpu.VMEM((latents, width), f32)
    row_shape = jax.ShapeDtypeStruct((8, latents), f32)
    kept_decoder = resident(decoder)
    squares = pl.pallas_call(
        squares_kernel, out_shape=lanes, in_specs=[ONCHIP], out_specs=ONCHIP, compiler_params=limit(8)
    )(resident(after(decoder, near)))
    early = pl.pallas_call(
        early_kernel,
        out_shape=kept_slab,
        in_specs=[ONCHIP] + [OUTSIDE] * 8,
        out_specs=ONCHIP,
        scratch_shapes=[pltpu.VMEM((5 * tokens, width), jnp.bfloat16), pltpu.SemaphoreType.DMA((8,))],
        compiler_params=limit(10),
        cost_estimate=pl.CostEstimate(flops=20 * latents * tokens * width, bytes_accessed=16 * latents * width, transcendentals=0),
    )(codes, *map(outside, (errors, near, *end2, *mid2, *mid3)))
    gradient, sums = pl.pallas_call(
        along_kernel,
        out_shape=(kept_slab, row_shape),
        in_specs=[ONCHIP] * 6,
        out_specs=(ONCHIP,) * 2,
        scratch_shapes=[pltpu.VMEM((latents, LANES), f32)],
        input_output_aliases={3: 0},
        compiler_params=limit(8),
    )(late_codes, resident(end3[0]), resident(end3[1]), resident(early), kept_decoder, squares)

    kept_gradient, kept_second = resident(gradient), resident(second_moment)
    out_sems = pltpu.SemaphoreType.DMA((latents // PART,))
    moved, ratio, lengths, new_first = pl.pallas_call(
        move_kernel,
        out_shape=(kept_slab, lanes, row_shape, slab),
        in_specs=[ONCHIP] * 8,
        out_specs=(ONCHIP,) * 3 + (OUTSIDE,),
        scratch_shapes=[pltpu.VMEM((latents, LANES), f32), pltpu.VMEM((latents, width), f32), out_sems],
        compiler_params=limit(8),
    )(*shares(sums), kept_gradient, kept_decoder, resident(first_moment), kept_second)
    new_second = pl.pallas_call(
        second_kernel,
        out_shape=slab,
        in_specs=[ONCHIP] * 4,
        out_specs=OUTSIDE,
        scratch_shapes=[pltpu.VMEM((latents, width), f32), out_sems],
        compiler_params=limit(8),
        cost_estimate=pl.CostEstimate(flops=10 * latents * width, bytes_accessed=8 * latents * width, transcendentals=0),
    )(ratio, kept_gradient, kept_decoder, kept_second)

    new_decoder = pl.pallas_call(
        unit_kernel,
        out_shape=slab,
        in_specs=[ONCHIP] * 5,
        out_specs=OUTSIDE,
        scratch_shapes=[pltpu.VMEM((latents, width), f32), out_sems],
        compiler_params=limit(8),
    )(*shares(lengths), resident(moved))
    return (new_decoder, new_first, new_second)


def gather_body(errors, block_ids, code_values, decoder, first_moment, second_moment):
    here = lax.axis_index("lat")
    lat_dev = decoder.shape[0]
    blk_dev = lat_dev // BLOCK
    every_ids = lax.all_gather(block_ids, "lat", axis=0, tiled=True)
    owned = here * blk_dev + jnp.arange(blk_dev, dtype=jnp.int32)
    err_piece = lax.all_gather(errors, "lat", axis=0, tiled=True)
    code_piece = lax.all_gather(code_values, "lat", axis=0, tiled=True)
    count = err_piece.shape[0]
    dense = jnp.zeros((count, blk_dev, BLOCK), jnp.bfloat16)
    for position in range(KB):
        match = every_ids[:, position][:, None] == owned[None, :]
        dense = dense + jnp.where(
            match[:, :, None], code_piece[:, position][:, None, :], jnp.zeros((), jnp.bfloat16)
        )
    dense = dense.reshape(count, blk_dev * BLOCK)
    gradient = lax.dot_general(
        dense, err_piece, (((0,), (0,)), ((), ())), preferred_element_type=jnp.float32
    )
    along, row_squares = lax.psum(
        (jnp.sum(gradient * decoder, axis=1), jnp.sum(decoder * decoder, axis=1)), "wid"
    )
    projected = gradient - (along / (row_squares + norm_epsilon))[:, None] * decoder
    new_first = beta_first * first_moment + (1.0 - beta_first) * projected
    new_second = beta_second * second_moment + (1.0 - beta_second) * projected * projected
    moved = decoder - learn_rate * (new_first / (1.0 - beta_first**ADAM_STEP)) / (
        jnp.sqrt(new_second / (1.0 - beta_second**ADAM_STEP)) + adam_epsilon
    )
    length_sq = lax.psum(jnp.sum(moved * moved, axis=1), "wid")
    new_decoder = moved / jnp.sqrt(length_sq + norm_epsilon)[:, None]
    return (new_decoder, new_first, new_second)


def solution(mesh):
    chain = mesh.shape["lat"] == 4 and mesh.shape["wid"] == 4
    in_specs = (
        P(("groups", "lat"), "wid"),
        P(("groups", "lat"), None),
        P(("groups", "lat"), None, None),
        P(("groups", "lat"), "wid"),
        P(("groups", "lat"), "wid"),
        P(("groups", "lat"), "wid"),
    )
    out_specs = (
        P(("groups", "lat"), "wid"),
        P(("groups", "lat"), "wid"),
        P(("groups", "lat"), "wid"),
    )
    body = chain_body if chain else gather_body
    return jax.shard_map(body, mesh=mesh, in_specs=in_specs, out_specs=out_specs, check_vma=False)
```

```python
import jax
import jax.numpy as jnp
from jax import lax
from jax.experimental import pallas as pl
from jax.experimental.pallas import tpu as pltpu
from jax.sharding import PartitionSpec as P

KB = 4
BLOCK = 128
ADAM_STEP = 100


beta_first = 0.9
beta_second = 0.999
learn_rate = 0.001
adam_epsilon = 1e-08
norm_epsilon = 1e-06

first_scale = 1.0 / (1.0 - beta_first**ADAM_STEP)
second_scale = 1.0 / (1.0 - beta_second**ADAM_STEP)

LANES = 128
MOST = 128
WIDE_BITS = (0, 2, 3, 1)
PAIR = ((0, 1), (1, 0), (2, 3), (3, 2))
MIDDLE = ((1, 2), (2, 1))
OUTWARD = ((1, 0), (2, 3))
f32 = jnp.float32


def after(value, *earlier):
    return lax.optimization_barrier((value,) + earlier)[0]


def swap(value, axis, size, bit):
    return lax.ppermute(value, axis, [(i, i ^ bit) for i in range(size)])


def row_of(lanes):
    return jnp.sum(lanes.T, axis=0, keepdims=True)


def column_of(row):
    return jnp.broadcast_to(row, (LANES, row.shape[1])).T


def fold(block):
    total = block[:, :LANES]
    for left in range(LANES, block.shape[1], LANES):
        total = total + block[:, left : left + LANES]
    return total


def pack_kernel(place_ref, ids_ref, codes_ref, out_ref):
    positions, tokens = ids_ref.shape
    names = [ids_ref[k : k + 1, :] for k in range(positions)]
    values = [codes_ref[k].astype(f32) for k in range(positions)]
    earlier = lax.broadcasted_iota(jnp.int32, (tokens, tokens), 0) < lax.broadcasted_iota(jnp.int32, (tokens, tokens), 1)
    earlier = earlier.astype(f32).astype(jnp.bfloat16)
    slots = lax.broadcasted_iota(jnp.int32, (MOST, tokens), 0).astype(f32)
    numbers = lax.broadcasted_iota(jnp.int32, (8, tokens), 1).astype(f32).astype(jnp.bfloat16)
    by_last = (((1,), (1,)), ((), ()))
    for owner in range(out_ref.shape[0]):
        block = owner * positions + place_ref[1]
        total = jnp.zeros((BLOCK, tokens), f32)
        named = jnp.zeros((1, tokens), f32)
        for name, value in zip(names, values):
            match = name == block
            total = total + jnp.where(match, value, 0.0)
            named = named + jnp.where(match, 1.0, 0.0)
        before = jnp.dot(
            jnp.broadcast_to(named, (8, tokens)).astype(jnp.bfloat16), earlier, preferred_element_type=f32
        )[:1]
        place = jnp.where(named > 0.0, before, -1.0)
        chosen = jnp.where(slots == place, 1.0, 0.0).astype(jnp.bfloat16)
        packed = lax.dot_general(total.astype(jnp.bfloat16), chosen, by_last, preferred_element_type=f32)
        out_ref[owner, :BLOCK, :] = packed.astype(jnp.bfloat16)
        whose = lax.dot_general(numbers, chosen, by_last, preferred_element_type=f32)
        out_ref[owner, BLOCK:, :] = whose.astype(jnp.bfloat16)


def dense_kernel(place_ref, *refs):
    *packed_refs, out_ref = refs
    count = packed_refs[0].shape[0]
    tokens = out_ref.shape[1] // count
    numbers = lax.broadcasted_iota(jnp.int32, (MOST, LANES), 1).astype(f32)
    for packed_ref, bit in zip(packed_refs, WIDE_BITS):
        block = place_ref[1] ^ bit
        rows = pl.ds(pl.multiple_of(block * BLOCK, BLOCK), BLOCK)
        for order in range(count):
            source = place_ref[0] ^ order
            whose = column_of(packed_ref[source, BLOCK:, :].astype(f32)[:1])
            for left in range(0, tokens, LANES):
                chosen = jnp.where(whose == numbers + float(left), 1.0, 0.0).astype(jnp.bfloat16)
                spread = jnp.dot(packed_ref[source, :BLOCK, :], chosen, preferred_element_type=f32)
                top = order * tokens + left
                out_ref[rows, top : top + LANES] = spread.astype(jnp.bfloat16)


def squares_kernel(decoder_ref, out_ref):
    chunk = 8

    def step(index, carry):
        rows = pl.ds(pl.multiple_of(index * chunk, chunk), chunk)
        weights = decoder_ref[rows, :]
        out_ref[rows, :] = fold(weights * weights)
        return carry

    lax.fori_loop(0, out_ref.shape[0] // chunk, step, 0, unroll=2)


def early_kernel(codes_ref, *refs):
    *piece_refs, grad_ref, rows_ref, sems = refs
    width = grad_ref.shape[1]
    copies, top = [], 0
    for index, piece in enumerate(piece_refs):
        high = piece.shape[0]
        copies.append(
            pltpu.make_async_copy(
                piece.at[:, pl.ds(0, width)], rows_ref.at[pl.ds(top, high)], sems.at[index]
            )
        )
        copies[-1].start()
        top += high
    for copy in copies:
        copy.wait()
    block = 512
    tokens = codes_ref.shape[1] // 4
    for left in range(0, width, block):
        columns = slice(left, left + block)
        grad_ref[:, columns] = jnp.dot(
            codes_ref[:, : 3 * tokens], rows_ref[: 3 * tokens, columns], preferred_element_type=f32
        ) + jnp.dot(codes_ref[:, 2 * tokens :], rows_ref[3 * tokens :, columns], preferred_element_type=f32)


def along_kernel(codes_ref, last0_ref, last1_ref, early_ref, decoder_ref, squares_ref, grad_ref, out_ref, total_ref):
    late_codes = codes_ref[:, codes_ref.shape[1] // 4 * 3 :]
    block = 512
    for left in range(0, grad_ref.shape[1], block):
        columns = slice(left, left + block)
        rows = jnp.concatenate([last0_ref[:, columns], last1_ref[:, columns]], axis=0)
        grad_ref[:, columns] = early_ref[:, columns] + jnp.dot(late_codes, rows, preferred_element_type=f32)
    chunk = 8

    def step(index, carry):
        rows = pl.ds(pl.multiple_of(index * chunk, chunk), chunk)
        total_ref[rows, :] = fold(grad_ref[rows, :] * decoder_ref[rows, :])
        return carry

    lax.fori_loop(0, grad_ref.shape[0] // chunk, step, 0, unroll=2)
    out_ref[0:1, :] = row_of(total_ref[...])
    out_ref[1:2, :] = row_of(squares_ref[...])


def ratio_of(sum0_ref, sum1_ref, sum2_ref, sum3_ref):
    sums = (sum0_ref[0:2, :] + sum1_ref[0:2, :]) + (sum2_ref[0:2, :] + sum3_ref[0:2, :])
    return column_of(sums[0:1] / (sums[1:2] + norm_epsilon))


def second_of(projected, second):
    return beta_second * second + ((1.0 - beta_second) * projected) * projected


PART = 64


def rows_out(buf, target, sems):
    parts = [pl.ds(index * PART, PART) for index in range(buf.shape[0] // PART)]
    return [pltpu.make_async_copy(buf.at[rows], target.at[rows], sems.at[i]) for i, rows in enumerate(parts)]


def move_kernel(sum0_ref, sum1_ref, sum2_ref, sum3_ref, grad_ref, decoder_ref, first_ref, second_ref,
                moved_ref, ratio_ref, out_ref, new_first_ref, total_ref, first_buf, sems):
    ratio_ref[...] = ratio_of(sum0_ref, sum1_ref, sum2_ref, sum3_ref)
    width = grad_ref.shape[1]
    chunk = 8
    copies = rows_out(first_buf, new_first_ref, sems)
    for index, copy in enumerate(copies):

        def step(inner, carry):
            rows = pl.ds(pl.multiple_of(index * PART + inner * chunk, chunk), chunk)
            ratio = ratio_ref[rows, :]
            total = jnp.zeros((chunk, LANES), f32)
            for left in range(0, width, LANES):
                columns = slice(left, left + LANES)
                weights = decoder_ref[rows, columns]
                projected = grad_ref[rows, columns] - ratio * weights
                new_first = beta_first * first_ref[rows, columns] + (1.0 - beta_first) * projected
                first_buf[rows, columns] = new_first
                new_second = second_of(projected, second_ref[rows, columns])
                unbiased = new_second * second_scale
                spread = unbiased * lax.rsqrt(unbiased) + adam_epsilon
                moved = weights - (learn_rate * first_scale) * new_first / spread
                moved_ref[rows, columns] = moved
                total = total + moved * moved
            total_ref[rows, :] = total
            return carry

        lax.fori_loop(0, PART // chunk, step, 0, unroll=PART // chunk)
        copy.start()
    out_ref[0:1, :] = row_of(total_ref[...])
    for copy in copies:
        copy.wait()


def second_kernel(ratio_ref, grad_ref, decoder_ref, second_ref, new_second_ref, second_buf, sems):
    width = grad_ref.shape[1]
    chunk = 8
    copies = rows_out(second_buf, new_second_ref, sems)
    for index, copy in enumerate(copies):

        def step(inner, carry):
            rows = pl.ds(pl.multiple_of(index * PART + inner * chunk, chunk), chunk)
            ratio = ratio_ref[rows, :]
            for left in range(0, width, LANES):
                columns = slice(left, left + LANES)
                projected = grad_ref[rows, columns] - ratio * decoder_ref[rows, columns]
                second_buf[rows, columns] = second_of(projected, second_ref[rows, columns])
            return carry

        lax.fori_loop(0, PART // chunk, step, 0, unroll=4)
        copy.start()
    for copy in copies:
        copy.wait()


def unit_kernel(sum0_ref, sum1_ref, sum2_ref, sum3_ref, moved_ref, out_ref, buf, sems):
    length = (sum0_ref[0:1, :] + sum1_ref[0:1, :]) + (sum2_ref[0:1, :] + sum3_ref[0:1, :])
    scale = column_of(1.0 / jnp.sqrt(length + norm_epsilon))
    width = moved_ref.shape[1]
    copies = rows_out(buf, out_ref, sems)
    for index, copy in enumerate(copies):
        rows = slice(index * PART, (index + 1) * PART)
        for left in range(0, width, LANES):
            buf[rows, left : left + LANES] = moved_ref[rows, left : left + LANES] * scale[rows]
        copy.start()
    for copy in copies:
        copy.wait()


SCALARS = pl.BlockSpec(memory_space=pltpu.SMEM)
ONCHIP = pl.BlockSpec(memory_space=pltpu.VMEM)
OUTSIDE = pl.BlockSpec(memory_space=pl.ANY)


def resident(value):
    return pltpu.with_memory_space_constraint(value, pltpu.VMEM)


def outside(value):
    return pltpu.with_memory_space_constraint(value, pltpu.HBM)


def limit(mib):
    return pltpu.CompilerParams(vmem_limit_bytes=mib * 1024 * 1024)


def shares(value):
    return [value] + [swap(value, "wid", 4, bit) for bit in WIDE_BITS[1:]]


def chain_body(errors, block_ids, code_values, decoder, first_moment, second_moment):
    here = lax.axis_index("lat")
    wide = lax.axis_index("wid")
    place = jnp.stack([here, wide]).astype(jnp.int32)
    tokens, width = errors.shape
    half = tokens // 2
    latents = decoder.shape[0]

    hop = lambda value, pairs: lax.ppermute(value, "lat", pairs)
    near = hop(errors, PAIR)
    packed = pl.pallas_call(
        pack_kernel,
        out_shape=jax.ShapeDtypeStruct((4, BLOCK + 8, MOST), jnp.bfloat16),
        in_specs=[SCALARS] + [ONCHIP] * 2,
        out_specs=ONCHIP,
        compiler_params=limit(8),
    )(place, block_ids.T, code_values.transpose(1, 2, 0))
    packed = lax.all_to_all(packed, "lat", 0, 0, tiled=True)

    mid3 = [hop(errors[i * half : (i + 1) * half], MIDDLE) for i in range(2)]
    end2 = [hop(part, OUTWARD) for part in mid3]
    near = after(near, mid3[0])
    mid2 = [hop(near[:half], MIDDLE), hop(after(near, mid3[1], packed)[half:], MIDDLE)]
    end3 = [hop(after(mid2[0], end2[0]), OUTWARD), hop(mid2[1], OUTWARD)]

    packed = after(packed, mid3[1])
    codes = pl.pallas_call(
        dense_kernel,
        out_shape=jax.ShapeDtypeStruct((latents, 4 * tokens), jnp.bfloat16),
        in_specs=[SCALARS] + [ONCHIP] * 4,
        out_specs=ONCHIP,
        compiler_params=limit(8),
    )(place, *shares(packed))

    lanes = jax.ShapeDtypeStruct((latents, LANES), f32)
    slab = jax.ShapeDtypeStruct((latents, width), f32)
    kept_slab = pltpu.VMEM((latents, width), f32)
    row_shape = jax.ShapeDtypeStruct((8, latents), f32)
    kept_decoder = resident(decoder)
    squares = pl.pallas_call(
        squares_kernel, out_shape=lanes, in_specs=[ONCHIP], out_specs=ONCHIP, compiler_params=limit(8)
    )(resident(after(decoder, near)))
    early = pl.pallas_call(
        early_kernel,
        out_shape=kept_slab,
        in_specs=[ONCHIP] + [OUTSIDE] * 8,
        out_specs=ONCHIP,
        scratch_shapes=[pltpu.VMEM((5 * tokens, width), jnp.bfloat16), pltpu.SemaphoreType.DMA((8,))],
        compiler_params=limit(10),
        cost_estimate=pl.CostEstimate(flops=20 * latents * tokens * width, bytes_accessed=16 * latents * width, transcendentals=0),
    )(codes, *map(outside, (errors, near, *end2, *mid2, *mid3)))
    gradient, sums = pl.pallas_call(
        along_kernel,
        out_shape=(kept_slab, row_shape),
        in_specs=[ONCHIP] * 6,
        out_specs=(ONCHIP,) * 2,
        scratch_shapes=[pltpu.VMEM((latents, LANES), f32)],
        input_output_aliases={3: 0},
        compiler_params=limit(8),
    )(codes, resident(end3[0]), resident(end3[1]), resident(early), kept_decoder, squares)

    kept_gradient, kept_second = resident(gradient), resident(second_moment)
    out_sems = pltpu.SemaphoreType.DMA((latents // PART,))
    moved, ratio, lengths, new_first = pl.pallas_call(
        move_kernel,
        out_shape=(kept_slab, lanes, row_shape, slab),
        in_specs=[ONCHIP] * 8,
        out_specs=(ONCHIP,) * 3 + (OUTSIDE,),
        scratch_shapes=[pltpu.VMEM((latents, LANES), f32), pltpu.VMEM((latents, width), f32), out_sems],
        compiler_params=limit(8),
    )(*shares(sums), kept_gradient, kept_decoder, resident(first_moment), kept_second)
    new_second = pl.pallas_call(
        second_kernel,
        out_shape=slab,
        in_specs=[ONCHIP] * 4,
        out_specs=OUTSIDE,
        scratch_shapes=[pltpu.VMEM((latents, width), f32), out_sems],
        compiler_params=limit(8),
        cost_estimate=pl.CostEstimate(flops=10 * latents * width, bytes_accessed=8 * latents * width, transcendentals=0),
    )(ratio, kept_gradient, kept_decoder, kept_second)

    new_decoder = pl.pallas_call(
        unit_kernel,
        out_shape=slab,
        in_specs=[ONCHIP] * 5,
        out_specs=OUTSIDE,
        scratch_shapes=[pltpu.VMEM((latents, width), f32), out_sems],
        compiler_params=limit(8),
    )(*shares(lengths), resident(moved))
    return (new_decoder, new_first, new_second)


def gather_body(errors, block_ids, code_values, decoder, first_moment, second_moment):
    here = lax.axis_index("lat")
    lat_dev = decoder.shape[0]
    blk_dev = lat_dev // BLOCK
    every_ids = lax.all_gather(block_ids, "lat", axis=0, tiled=True)
    owned = here * blk_dev + jnp.arange(blk_dev, dtype=jnp.int32)
    err_piece = lax.all_gather(errors, "lat", axis=0, tiled=True)
    code_piece = lax.all_gather(code_values, "lat", axis=0, tiled=True)
    count = err_piece.shape[0]
    dense = jnp.zeros((count, blk_dev, BLOCK), jnp.bfloat16)
    for position in range(KB):
        match = every_ids[:, position][:, None] == owned[None, :]
        dense = dense + jnp.where(
            match[:, :, None], code_piece[:, position][:, None, :], jnp.zeros((), jnp.bfloat16)
        )
    dense = dense.reshape(count, blk_dev * BLOCK)
    gradient = lax.dot_general(
        dense, err_piece, (((0,), (0,)), ((), ())), preferred_element_type=jnp.float32
    )
    along, row_squares = lax.psum(
        (jnp.sum(gradient * decoder, axis=1), jnp.sum(decoder * decoder, axis=1)), "wid"
    )
    projected = gradient - (along / (row_squares + norm_epsilon))[:, None] * decoder
    new_first = beta_first * first_moment + (1.0 - beta_first) * projected
    new_second = beta_second * second_moment + (1.0 - beta_second) * projected * projected
    moved = decoder - learn_rate * (new_first / (1.0 - beta_first**ADAM_STEP)) / (
        jnp.sqrt(new_second / (1.0 - beta_second**ADAM_STEP)) + adam_epsilon
    )
    length_sq = lax.psum(jnp.sum(moved * moved, axis=1), "wid")
    new_decoder = moved / jnp.sqrt(length_sq + norm_epsilon)[:, None]
    return (new_decoder, new_first, new_second)


def solution(mesh):
    chain = mesh.shape["lat"] == 4 and mesh.shape["wid"] == 4
    in_specs = (
        P(("groups", "lat"), "wid"),
        P(("groups", "lat"), None),
        P(("groups", "lat"), None, None),
        P(("groups", "lat"), "wid"),
        P(("groups", "lat"), "wid"),
        P(("groups", "lat"), "wid"),
    )
    out_specs = (
        P(("groups", "lat"), "wid"),
        P(("groups", "lat"), "wid"),
        P(("groups", "lat"), "wid"),
    )
    body = chain_body if chain else gather_body
    return jax.shard_map(body, mesh=mesh, in_specs=in_specs, out_specs=out_specs, check_vma=False)
```

```python
import jax
import jax.numpy as jnp
from jax import lax
from jax.experimental import pallas as pl
from jax.experimental.pallas import tpu as pltpu
from jax.sharding import PartitionSpec as P

KB = 4
BLOCK = 128
ADAM_STEP = 100


beta_first = 0.9
beta_second = 0.999
learn_rate = 0.001
adam_epsilon = 1e-08
norm_epsilon = 1e-06

first_scale = 1.0 / (1.0 - beta_first**ADAM_STEP)
second_scale = 1.0 / (1.0 - beta_second**ADAM_STEP)

LANES = 128
MOST = 128
WIDE_BITS = (0, 2, 3, 1)
PAIR = ((0, 1), (1, 0), (2, 3), (3, 2))
MIDDLE = ((1, 2), (2, 1))
OUTWARD = ((1, 0), (2, 3))
f32 = jnp.float32


def after(value, *earlier):
    return lax.optimization_barrier((value,) + earlier)[0]


def swap(value, axis, size, bit):
    return lax.ppermute(value, axis, [(i, i ^ bit) for i in range(size)])


def row_of(lanes):
    return jnp.sum(lanes.T, axis=0, keepdims=True)


def column_of(row):
    return jnp.broadcast_to(row, (LANES, row.shape[1])).T


def fold(block):
    total = block[:, :LANES]
    for left in range(LANES, block.shape[1], LANES):
        total = total + block[:, left : left + LANES]
    return total


def pack_kernel(place_ref, ids_ref, codes_ref, out_ref):
    positions, tokens = ids_ref.shape
    names = [ids_ref[k : k + 1, :] for k in range(positions)]
    values = [codes_ref[k].astype(f32) for k in range(positions)]
    earlier = lax.broadcasted_iota(jnp.int32, (tokens, tokens), 0) < lax.broadcasted_iota(jnp.int32, (tokens, tokens), 1)
    earlier = earlier.astype(f32).astype(jnp.bfloat16)
    slots = lax.broadcasted_iota(jnp.int32, (MOST, tokens), 0).astype(f32)
    numbers = lax.broadcasted_iota(jnp.int32, (16, tokens), 1).astype(f32).astype(jnp.bfloat16)
    by_last = (((1,), (1,)), ((), ()))
    for owner in range(out_ref.shape[0]):
        block = owner * positions + place_ref[1]
        total = jnp.zeros((BLOCK, tokens), f32)
        named = jnp.zeros((1, tokens), f32)
        for name, value in zip(names, values):
            match = name == block
            total = total + jnp.where(match, value, 0.0)
            named = named + jnp.where(match, 1.0, 0.0)
        before = jnp.dot(
            jnp.broadcast_to(named, (8, tokens)).astype(jnp.bfloat16), earlier, preferred_element_type=f32
        )[:1]
        place = jnp.where(named > 0.0, before, -1.0)
        chosen = jnp.where(slots == place, 1.0, 0.0).astype(jnp.bfloat16)
        packed = lax.dot_general(total.astype(jnp.bfloat16), chosen, by_last, preferred_element_type=f32)
        out_ref[owner, :BLOCK, :] = packed.astype(jnp.bfloat16)
        whose = lax.dot_general(numbers, chosen, by_last, preferred_element_type=f32)
        out_ref[owner, BLOCK:, :] = whose.astype(jnp.bfloat16)


def dense_kernel(place_ref, *refs):
    *packed_refs, out_ref = refs
    count = packed_refs[0].shape[0]
    tokens = out_ref.shape[1] // count
    numbers = lax.broadcasted_iota(jnp.int32, (MOST, LANES), 1).astype(f32)
    for packed_ref, bit in zip(packed_refs, WIDE_BITS):
        block = place_ref[1] ^ bit
        rows = pl.ds(pl.multiple_of(block * BLOCK, BLOCK), BLOCK)
        for order in range(count):
            source = place_ref[0] ^ order
            whose = column_of(packed_ref[source, BLOCK:, :].astype(f32)[:1])
            for left in range(0, tokens, LANES):
                chosen = jnp.where(whose == numbers + float(left), 1.0, 0.0).astype(jnp.bfloat16)
                spread = jnp.dot(packed_ref[source, :BLOCK, :], chosen, preferred_element_type=f32)
                top = order * tokens + left
                out_ref[rows, top : top + LANES] = spread.astype(jnp.bfloat16)


def squares_kernel(decoder_ref, out_ref, lanes_ref):
    chunk = 8

    def step(index, carry):
        rows = pl.ds(pl.multiple_of(index * chunk, chunk), chunk)
        weights = decoder_ref[rows, :]
        lanes_ref[rows, :] = fold(weights * weights)
        return carry

    lax.fori_loop(0, lanes_ref.shape[0] // chunk, step, 0, unroll=2)
    out_ref[...] = row_of(lanes_ref[...])


def early_kernel(codes_ref, *refs):
    *piece_refs, grad_ref, rows_ref, sems = refs
    width = grad_ref.shape[1]
    copies, top = [], 0
    for index, piece in enumerate(piece_refs):
        high = piece.shape[0]
        copies.append(
            pltpu.make_async_copy(
                piece.at[:, pl.ds(0, width)], rows_ref.at[pl.ds(top, high)], sems.at[index]
            )
        )
        copies[-1].start()
        top += high
    for copy in copies:
        copy.wait()
    block = 512
    tokens = codes_ref.shape[1] // 4
    for left in range(0, width, block):
        columns = slice(left, left + block)
        grad_ref[:, columns] = jnp.dot(
            codes_ref[:, : 3 * tokens], rows_ref[: 3 * tokens, columns], preferred_element_type=f32
        ) + jnp.dot(codes_ref[:, 2 * tokens :], rows_ref[3 * tokens :, columns], preferred_element_type=f32)


def along_kernel(codes_ref, last0_ref, last1_ref, early_ref, decoder_ref, squares_ref, grad_ref, out_ref, total_ref):
    late_codes = codes_ref[:, codes_ref.shape[1] // 4 * 3 :]
    block = 512
    for left in range(0, grad_ref.shape[1], block):
        columns = slice(left, left + block)
        rows = jnp.concatenate([last0_ref[:, columns], last1_ref[:, columns]], axis=0)
        gradient = early_ref[:, columns] + jnp.dot(late_codes, rows, preferred_element_type=f32)
        grad_ref[:, columns] = gradient
        share = fold(gradient * decoder_ref[:, columns])
        total_ref[...] = share if left == 0 else total_ref[...] + share
    out_ref[0:1, :] = row_of(total_ref[...])
    out_ref[1:2, :] = squares_ref[...]


def ratio_of(sum0_ref, sum1_ref, sum2_ref, sum3_ref):
    sums = (sum0_ref[...] + sum1_ref[...]) + (sum2_ref[...] + sum3_ref[...])
    return column_of(sums[0:1] / (sums[1:2] + norm_epsilon))


PART = 64


def rows_out(buf, target, sems):
    parts = [pl.ds(index * PART, PART) for index in range(buf.shape[0] // PART)]
    return [pltpu.make_async_copy(buf.at[rows], target.at[rows], sems.at[i]) for i, rows in enumerate(parts)]


def scale_kernel(first_ref, second_ref, scaled_first_ref, scaled_second_ref):
    chunk = 8

    def step(index, carry):
        rows = pl.ds(pl.multiple_of(index * chunk, chunk), chunk)
        scaled_first_ref[rows, :] = beta_first * first_ref[rows, :]
        scaled_second_ref[rows, :] = (beta_second * second_scale) * second_ref[rows, :]
        return carry

    lax.fori_loop(0, first_ref.shape[0] // chunk, step, 0, unroll=2)


def move_kernel(sum0_ref, sum1_ref, sum2_ref, sum3_ref, grad_ref, decoder_ref, scaled_first_ref, scaled_second_ref,
                moved_ref, ratio_ref, out_ref, new_first_ref, total_ref, first_buf, sems):
    ratio_ref[...] = ratio_of(sum0_ref, sum1_ref, sum2_ref, sum3_ref)
    width = grad_ref.shape[1]
    chunk = 8
    copies = rows_out(first_buf, new_first_ref, sems)
    for index, copy in enumerate(copies):

        def step(inner, carry):
            rows = pl.ds(pl.multiple_of(index * PART + inner * chunk, chunk), chunk)
            ratio = ratio_ref[rows, :]
            total = jnp.zeros((chunk, LANES), f32)
            for left in range(0, width, LANES):
                columns = slice(left, left + LANES)
                weights = decoder_ref[rows, columns]
                projected = grad_ref[rows, columns] - ratio * weights
                new_first = scaled_first_ref[rows, columns] + (1.0 - beta_first) * projected
                first_buf[rows, columns] = new_first
                unbiased = scaled_second_ref[rows, columns] + ((1.0 - beta_second) * second_scale) * (projected * projected)
                spread = unbiased * lax.rsqrt(unbiased) + adam_epsilon
                moved = weights - (learn_rate * first_scale) * new_first / spread
                moved_ref[rows, columns] = moved
                total = total + moved * moved
            total_ref[rows, :] = total
            return carry

        lax.fori_loop(0, PART // chunk, step, 0, unroll=PART // chunk)
        copy.start()
    out_ref[...] = row_of(total_ref[...])
    for copy in copies:
        copy.wait()


def second_kernel(ratio_ref, grad_ref, decoder_ref, second_ref, new_second_ref, second_buf, sems):
    width = grad_ref.shape[1]
    chunk = 8
    copies = rows_out(second_buf, new_second_ref, sems)
    for index, copy in enumerate(copies):

        def step(inner, carry):
            rows = pl.ds(pl.multiple_of(index * PART + inner * chunk, chunk), chunk)
            ratio = ratio_ref[rows, :]
            for left in range(0, width, LANES):
                columns = slice(left, left + LANES)
                projected = grad_ref[rows, columns] - ratio * decoder_ref[rows, columns]
                second = second_ref[rows, columns]
                second_buf[rows, columns] = beta_second * second + ((1.0 - beta_second) * projected) * projected
            return carry

        lax.fori_loop(0, PART // chunk, step, 0, unroll=4)
        copy.start()
    for copy in copies:
        copy.wait()


def unit_kernel(sum0_ref, sum1_ref, sum2_ref, sum3_ref, moved_ref, out_ref, buf, sems):
    length = (sum0_ref[...] + sum1_ref[...]) + (sum2_ref[...] + sum3_ref[...])
    scale = column_of(1.0 / jnp.sqrt(length + norm_epsilon))
    width = moved_ref.shape[1]
    copies = rows_out(buf, out_ref, sems)
    for index, copy in enumerate(copies):
        rows = slice(index * PART, (index + 1) * PART)
        for left in range(0, width, LANES):
            buf[rows, left : left + LANES] = moved_ref[rows, left : left + LANES] * scale[rows]
        copy.start()
    for copy in copies:
        copy.wait()


SCALARS = pl.BlockSpec(memory_space=pltpu.SMEM)
ONCHIP = pl.BlockSpec(memory_space=pltpu.VMEM)
OUTSIDE = pl.BlockSpec(memory_space=pl.ANY)


def resident(value):
    return pltpu.with_memory_space_constraint(value, pltpu.VMEM)


def outside(value):
    return pltpu.with_memory_space_constraint(value, pltpu.HBM)


def limit(mib):
    return pltpu.CompilerParams(vmem_limit_bytes=mib * 1024 * 1024)


def shares(value):
    return [value] + [swap(value, "wid", 4, bit) for bit in WIDE_BITS[1:]]


def chain_body(errors, block_ids, code_values, decoder, first_moment, second_moment):
    here = lax.axis_index("lat")
    wide = lax.axis_index("wid")
    place = jnp.stack([here, wide]).astype(jnp.int32)
    tokens, width = errors.shape
    half = tokens // 2
    latents = decoder.shape[0]

    hop = lambda value, pairs: lax.ppermute(value, "lat", pairs)
    near = hop(errors, PAIR)
    packed = pl.pallas_call(
        pack_kernel,
        out_shape=jax.ShapeDtypeStruct((4, BLOCK + 16, MOST), jnp.bfloat16),
        in_specs=[SCALARS] + [ONCHIP] * 2,
        out_specs=ONCHIP,
        compiler_params=limit(8),
    )(place, block_ids.T, code_values.transpose(1, 2, 0))
    packed = lax.all_to_all(packed, "lat", 0, 0, tiled=True)

    mid3 = [hop(errors[i * half : (i + 1) * half], MIDDLE) for i in range(2)]
    end2 = [hop(part, OUTWARD) for part in mid3]
    near = after(near, mid3[0])
    mid2 = [hop(near[:half], MIDDLE), hop(after(near, mid3[1], packed)[half:], MIDDLE)]
    end3 = [hop(after(mid2[0], end2[0]), OUTWARD), hop(mid2[1], OUTWARD)]

    packed = after(packed, mid3[1])
    codes = pl.pallas_call(
        dense_kernel,
        out_shape=jax.ShapeDtypeStruct((latents, 4 * tokens), jnp.bfloat16),
        in_specs=[SCALARS] + [ONCHIP] * 4,
        out_specs=ONCHIP,
        compiler_params=limit(8),
    )(place, *shares(packed))

    lanes = jax.ShapeDtypeStruct((latents, LANES), f32)
    slab = jax.ShapeDtypeStruct((latents, width), f32)
    kept_slab = pltpu.VMEM((latents, width), f32)
    kept_decoder = resident(decoder)
    squares = pl.pallas_call(
        squares_kernel,
        out_shape=jax.ShapeDtypeStruct((1, latents), f32),
        in_specs=[ONCHIP],
        out_specs=ONCHIP,
        scratch_shapes=[pltpu.VMEM((latents, LANES), f32)],
        compiler_params=limit(8),
    )(resident(after(decoder, near)))
    early = pl.pallas_call(
        early_kernel,
        out_shape=kept_slab,
        in_specs=[ONCHIP] + [OUTSIDE] * 8,
        out_specs=ONCHIP,
        scratch_shapes=[pltpu.VMEM((5 * tokens, width), jnp.bfloat16), pltpu.SemaphoreType.DMA((8,))],
        compiler_params=limit(10),
        cost_estimate=pl.CostEstimate(flops=20 * latents * tokens * width, bytes_accessed=16 * latents * width, transcendentals=0),
    )(codes, *map(outside, (errors, near, *end2, *mid2, *mid3)))
    gradient, sums = pl.pallas_call(
        along_kernel,
        out_shape=(kept_slab, jax.ShapeDtypeStruct((2, latents), f32)),
        in_specs=[ONCHIP] * 6,
        out_specs=(ONCHIP,) * 2,
        scratch_shapes=[pltpu.VMEM((latents, LANES), f32)],
        input_output_aliases={3: 0},
        compiler_params=limit(8),
    )(codes, resident(end3[0]), resident(end3[1]), resident(early), kept_decoder, squares)

    scaled_first, scaled_second = pl.pallas_call(
        scale_kernel,
        out_shape=(kept_slab, kept_slab),
        in_specs=[ONCHIP] * 2,
        out_specs=(ONCHIP,) * 2,
        compiler_params=limit(4),
    )(resident(after(first_moment, mid2[0])), resident(after(second_moment, mid2[0])))
    kept_gradient = resident(gradient)
    out_sems = pltpu.SemaphoreType.DMA((latents // PART,))
    moved, ratio, lengths, new_first = pl.pallas_call(
        move_kernel,
        out_shape=(kept_slab, lanes, jax.ShapeDtypeStruct((1, latents), f32), slab),
        in_specs=[ONCHIP] * 8,
        out_specs=(ONCHIP,) * 3 + (OUTSIDE,),
        scratch_shapes=[pltpu.VMEM((latents, LANES), f32), pltpu.VMEM((latents, width), f32), out_sems],
        compiler_params=limit(8),
    )(*shares(sums), kept_gradient, kept_decoder, resident(scaled_first), resident(scaled_second))
    new_second = pl.pallas_call(
        second_kernel,
        out_shape=slab,
        in_specs=[ONCHIP] * 4,
        out_specs=OUTSIDE,
        scratch_shapes=[pltpu.VMEM((latents, width), f32), out_sems],
        compiler_params=limit(8),
        cost_estimate=pl.CostEstimate(flops=10 * latents * width, bytes_accessed=8 * latents * width, transcendentals=0),
    )(ratio, kept_gradient, kept_decoder, resident(second_moment))

    new_decoder = pl.pallas_call(
        unit_kernel,
        out_shape=slab,
        in_specs=[ONCHIP] * 5,
        out_specs=OUTSIDE,
        scratch_shapes=[pltpu.VMEM((latents, width), f32), out_sems],
        compiler_params=limit(8),
    )(*shares(lengths), resident(moved))
    return (new_decoder, new_first, new_second)


def gather_body(errors, block_ids, code_values, decoder, first_moment, second_moment):
    here = lax.axis_index("lat")
    lat_dev = decoder.shape[0]
    blk_dev = lat_dev // BLOCK
    every_ids = lax.all_gather(block_ids, "lat", axis=0, tiled=True)
    owned = here * blk_dev + jnp.arange(blk_dev, dtype=jnp.int32)
    err_piece = lax.all_gather(errors, "lat", axis=0, tiled=True)
    code_piece = lax.all_gather(code_values, "lat", axis=0, tiled=True)
    count = err_piece.shape[0]
    dense = jnp.zeros((count, blk_dev, BLOCK), jnp.bfloat16)
    for position in range(KB):
        match = every_ids[:, position][:, None] == owned[None, :]
        dense = dense + jnp.where(
            match[:, :, None], code_piece[:, position][:, None, :], jnp.zeros((), jnp.bfloat16)
        )
    dense = dense.reshape(count, blk_dev * BLOCK)
    gradient = lax.dot_general(
        dense, err_piece, (((0,), (0,)), ((), ())), preferred_element_type=jnp.float32
    )
    along, row_squares = lax.psum(
        (jnp.sum(gradient * decoder, axis=1), jnp.sum(decoder * decoder, axis=1)), "wid"
    )
    projected = gradient - (along / (row_squares + norm_epsilon))[:, None] * decoder
    new_first = beta_first * first_moment + (1.0 - beta_first) * projected
    new_second = beta_second * second_moment + (1.0 - beta_second) * projected * projected
    moved = decoder - learn_rate * (new_first / (1.0 - beta_first**ADAM_STEP)) / (
        jnp.sqrt(new_second / (1.0 - beta_second**ADAM_STEP)) + adam_epsilon
    )
    length_sq = lax.psum(jnp.sum(moved * moved, axis=1), "wid")
    new_decoder = moved / jnp.sqrt(length_sq + norm_epsilon)[:, None]
    return (new_decoder, new_first, new_second)


def solution(mesh):
    chain = mesh.shape["lat"] == 4 and mesh.shape["wid"] == 4
    in_specs = (
        P(("groups", "lat"), "wid"),
        P(("groups", "lat"), None),
        P(("groups", "lat"), None, None),
        P(("groups", "lat"), "wid"),
        P(("groups", "lat"), "wid"),
        P(("groups", "lat"), "wid"),
    )
    out_specs = (
        P(("groups", "lat"), "wid"),
        P(("groups", "lat"), "wid"),
        P(("groups", "lat"), "wid"),
    )
    body = chain_body if chain else gather_body
    return jax.shard_map(body, mesh=mesh, in_specs=in_specs, out_specs=out_specs, check_vma=False)
```

```python
import jax
import jax.numpy as jnp
from jax import lax
from jax.experimental import pallas as pl
from jax.experimental.pallas import tpu as pltpu
from jax.sharding import PartitionSpec as P

KB = 4
BLOCK = 128
ADAM_STEP = 100


beta_first = 0.9
beta_second = 0.999
learn_rate = 0.001
adam_epsilon = 1e-08
norm_epsilon = 1e-06

first_scale = 1.0 / (1.0 - beta_first**ADAM_STEP)
second_scale = 1.0 / (1.0 - beta_second**ADAM_STEP)

LANES = 128
MOST = 128
WIDE_BITS = (0, 2, 3, 1)
PAIR = ((0, 1), (1, 0), (2, 3), (3, 2))
MIDDLE = ((1, 2), (2, 1))
OUTWARD = ((1, 0), (2, 3))
f32 = jnp.float32


def after(value, *earlier):
    return lax.optimization_barrier((value,) + earlier)[0]


def swap(value, axis, size, bit):
    return lax.ppermute(value, axis, [(i, i ^ bit) for i in range(size)])


def row_of(lanes):
    return jnp.sum(lanes.T, axis=0, keepdims=True)


def column_of(row):
    return jnp.broadcast_to(row, (LANES, row.shape[1])).T


def fold(block):
    total = block[:, :LANES]
    for left in range(LANES, block.shape[1], LANES):
        total = total + block[:, left : left + LANES]
    return total


def pack_kernel(place_ref, ids_ref, codes_ref, out_ref):
    positions, tokens = ids_ref.shape
    names = [ids_ref[k : k + 1, :] for k in range(positions)]
    values = [codes_ref[k].astype(f32) for k in range(positions)]
    earlier = lax.broadcasted_iota(jnp.int32, (tokens, tokens), 0) < lax.broadcasted_iota(jnp.int32, (tokens, tokens), 1)
    earlier = earlier.astype(f32).astype(jnp.bfloat16)
    slots = lax.broadcasted_iota(jnp.int32, (MOST, tokens), 0).astype(f32)
    numbers = lax.broadcasted_iota(jnp.int32, (16, tokens), 1).astype(f32).astype(jnp.bfloat16)
    by_last = (((1,), (1,)), ((), ()))
    for owner in range(out_ref.shape[0]):
        block = owner * positions + place_ref[1]
        total = jnp.zeros((BLOCK, tokens), f32)
        named = jnp.zeros((1, tokens), f32)
        for name, value in zip(names, values):
            match = name == block
            total = total + jnp.where(match, value, 0.0)
            named = named + jnp.where(match, 1.0, 0.0)
        before = jnp.dot(
            jnp.broadcast_to(named, (8, tokens)).astype(jnp.bfloat16), earlier, preferred_element_type=f32
        )[:1]
        place = jnp.where(named > 0.0, before, -1.0)
        chosen = jnp.where(slots == place, 1.0, 0.0).astype(jnp.bfloat16)
        packed = lax.dot_general(total.astype(jnp.bfloat16), chosen, by_last, preferred_element_type=f32)
        out_ref[owner, :BLOCK, :] = packed.astype(jnp.bfloat16)
        whose = lax.dot_general(numbers, chosen, by_last, preferred_element_type=f32)
        out_ref[owner, BLOCK:, :] = whose.astype(jnp.bfloat16)


def dense_kernel(place_ref, *refs):
    *packed_refs, out_ref = refs
    count = packed_refs[0].shape[0]
    tokens = out_ref.shape[1] // count
    numbers = lax.broadcasted_iota(jnp.int32, (MOST, LANES), 1).astype(f32)
    for packed_ref, bit in zip(packed_refs, WIDE_BITS):
        block = place_ref[1] ^ bit
        rows = pl.ds(pl.multiple_of(block * BLOCK, BLOCK), BLOCK)
        for order in range(count):
            source = place_ref[0] ^ order
            whose = column_of(packed_ref[source, BLOCK:, :].astype(f32)[:1])
            for left in range(0, tokens, LANES):
                chosen = jnp.where(whose == numbers + float(left), 1.0, 0.0).astype(jnp.bfloat16)
                spread = jnp.dot(packed_ref[source, :BLOCK, :], chosen, preferred_element_type=f32)
                top = order * tokens + left
                out_ref[rows, top : top + LANES] = spread.astype(jnp.bfloat16)


def squares_kernel(decoder_ref, out_ref, lanes_ref):
    chunk = 8

    def step(index, carry):
        rows = pl.ds(pl.multiple_of(index * chunk, chunk), chunk)
        weights = decoder_ref[rows, :]
        lanes_ref[rows, :] = fold(weights * weights)
        return carry

    lax.fori_loop(0, lanes_ref.shape[0] // chunk, step, 0, unroll=2)
    out_ref[...] = row_of(lanes_ref[...])


def early_kernel(codes_ref, *refs):
    *piece_refs, grad_ref, rows_ref, sems = refs
    width = grad_ref.shape[1]
    copies, top = [], 0
    for index, piece in enumerate(piece_refs):
        high = piece.shape[0]
        copies.append(
            pltpu.make_async_copy(
                piece.at[:, pl.ds(0, width)], rows_ref.at[pl.ds(top, high)], sems.at[index]
            )
        )
        copies[-1].start()
        top += high
    for copy in copies:
        copy.wait()
    block = 512
    tokens = codes_ref.shape[1] // 4
    for left in range(0, width, block):
        columns = slice(left, left + block)
        grad_ref[:, columns] = jnp.dot(
            codes_ref[:, : 3 * tokens], rows_ref[: 3 * tokens, columns], preferred_element_type=f32
        ) + jnp.dot(codes_ref[:, 2 * tokens :], rows_ref[3 * tokens :, columns], preferred_element_type=f32)


def along_kernel(codes_ref, last0_ref, last1_ref, early_ref, decoder_ref, squares_ref, grad_ref, out_ref, total_ref):
    late_codes = codes_ref[:, codes_ref.shape[1] // 4 * 3 :]
    block = 512
    for left in range(0, grad_ref.shape[1], block):
        columns = slice(left, left + block)
        rows = jnp.concatenate([last0_ref[:, columns], last1_ref[:, columns]], axis=0)
        gradient = early_ref[:, columns] + jnp.dot(late_codes, rows, preferred_element_type=f32)
        grad_ref[:, columns] = gradient
        share = fold(gradient * decoder_ref[:, columns])
        total_ref[...] = share if left == 0 else total_ref[...] + share
    out_ref[0:1, :] = row_of(total_ref[...])
    out_ref[1:2, :] = squares_ref[...]


def ratio_of(sum0_ref, sum1_ref, sum2_ref, sum3_ref):
    sums = (sum0_ref[...] + sum1_ref[...]) + (sum2_ref[...] + sum3_ref[...])
    return column_of(sums[0:1] / (sums[1:2] + norm_epsilon))


PART = 64


def rows_out(buf, target, sems):
    parts = [pl.ds(index * PART, PART) for index in range(buf.shape[0] // PART)]
    return [pltpu.make_async_copy(buf.at[rows], target.at[rows], sems.at[i]) for i, rows in enumerate(parts)]


def scale_kernel(first_ref, second_ref, scaled_first_ref, scaled_second_ref):
    chunk = 8

    def step(index, carry):
        rows = pl.ds(pl.multiple_of(index * chunk, chunk), chunk)
        scaled_first_ref[rows, :] = beta_first * first_ref[rows, :]
        scaled_second_ref[rows, :] = (beta_second * second_scale) * second_ref[rows, :]
        return carry

    lax.fori_loop(0, first_ref.shape[0] // chunk, step, 0, unroll=2)


def move_kernel(sum0_ref, sum1_ref, sum2_ref, sum3_ref, grad_ref, decoder_ref, scaled_first_ref, scaled_second_ref,
                moved_ref, ratio_ref, out_ref, new_first_ref, total_ref, first_buf, sems):
    ratio_ref[...] = ratio_of(sum0_ref, sum1_ref, sum2_ref, sum3_ref)
    width = grad_ref.shape[1]
    chunk = 8
    copies = rows_out(first_buf, new_first_ref, sems)
    for index, copy in enumerate(copies):

        def step(inner, carry):
            rows = pl.ds(pl.multiple_of(index * PART + inner * chunk, chunk), chunk)
            ratio = ratio_ref[rows, :]
            total = jnp.zeros((chunk, LANES), f32)
            for left in range(0, width, LANES):
                columns = slice(left, left + LANES)
                weights = decoder_ref[rows, columns]
                projected = grad_ref[rows, columns] - ratio * weights
                new_first = scaled_first_ref[rows, columns] + (1.0 - beta_first) * projected
                first_buf[rows, columns] = new_first
                unbiased = scaled_second_ref[rows, columns] + ((1.0 - beta_second) * second_scale) * (projected * projected)
                spread = unbiased * lax.rsqrt(unbiased) + adam_epsilon
                moved = weights - (learn_rate * first_scale) * new_first / spread
                moved_ref[rows, columns] = moved
                total = total + moved * moved
            total_ref[rows, :] = total
            return carry

        lax.fori_loop(0, PART // chunk, step, 0, unroll=PART // chunk)
        copy.start()
    out_ref[...] = row_of(total_ref[...])
    for copy in copies:
        copy.wait()


def second_kernel(ratio_ref, grad_ref, decoder_ref, second_ref, new_second_ref, second_buf, sems):
    width = grad_ref.shape[1]
    chunk = 8
    copies = rows_out(second_buf, new_second_ref, sems)
    for index, copy in enumerate(copies):

        def step(inner, carry):
            rows = pl.ds(pl.multiple_of(index * PART + inner * chunk, chunk), chunk)
            ratio = ratio_ref[rows, :]
            for left in range(0, width, LANES):
                columns = slice(left, left + LANES)
                projected = grad_ref[rows, columns] - ratio * decoder_ref[rows, columns]
                second = second_ref[rows, columns]
                second_buf[rows, columns] = beta_second * second + ((1.0 - beta_second) * projected) * projected
            return carry

        lax.fori_loop(0, PART // chunk, step, 0, unroll=4)
        copy.start()
    for copy in copies:
        copy.wait()


def unit_kernel(sum0_ref, sum1_ref, sum2_ref, sum3_ref, moved_ref, out_ref, buf, sems):
    length = (sum0_ref[...] + sum1_ref[...]) + (sum2_ref[...] + sum3_ref[...])
    scale = column_of(1.0 / jnp.sqrt(length + norm_epsilon))
    width = moved_ref.shape[1]
    copies = rows_out(buf, out_ref, sems)
    for index, copy in enumerate(copies):
        rows = slice(index * PART, (index + 1) * PART)
        for left in range(0, width, LANES):
            buf[rows, left : left + LANES] = moved_ref[rows, left : left + LANES] * scale[rows]
        copy.start()
    for copy in copies:
        copy.wait()


SCALARS = pl.BlockSpec(memory_space=pltpu.SMEM)
ONCHIP = pl.BlockSpec(memory_space=pltpu.VMEM)
OUTSIDE = pl.BlockSpec(memory_space=pl.ANY)


def resident(value):
    return pltpu.with_memory_space_constraint(value, pltpu.VMEM)


def outside(value):
    return pltpu.with_memory_space_constraint(value, pltpu.HBM)


def limit(mib):
    return pltpu.CompilerParams(vmem_limit_bytes=mib * 1024 * 1024)


def shares(value):
    return [value] + [swap(value, "wid", 4, bit) for bit in WIDE_BITS[1:]]


def chain_body(errors, block_ids, code_values, decoder, first_moment, second_moment):
    here = lax.axis_index("lat")
    wide = lax.axis_index("wid")
    place = jnp.stack([here, wide]).astype(jnp.int32)
    tokens, width = errors.shape
    half = tokens // 2
    latents = decoder.shape[0]

    hop = lambda value, pairs: lax.ppermute(value, "lat", pairs)
    near = hop(errors, PAIR)
    packed = pl.pallas_call(
        pack_kernel,
        out_shape=jax.ShapeDtypeStruct((4, BLOCK + 16, MOST), jnp.bfloat16),
        in_specs=[SCALARS] + [ONCHIP] * 2,
        out_specs=ONCHIP,
        compiler_params=limit(8),
    )(place, block_ids.T, code_values.transpose(1, 2, 0))
    packed = lax.all_to_all(packed, "lat", 0, 0, tiled=True)

    mid3 = [hop(errors[i * half : (i + 1) * half], MIDDLE) for i in range(2)]
    end2 = [hop(part, OUTWARD) for part in mid3]
    near = after(near, mid3[0])
    mid2 = [hop(near[:half], MIDDLE), hop(after(near, mid3[1], packed)[half:], MIDDLE)]
    end3 = [hop(after(mid2[0], end2[0]), OUTWARD), hop(mid2[1], OUTWARD)]

    packed = after(packed, mid3[1])
    codes = pl.pallas_call(
        dense_kernel,
        out_shape=jax.ShapeDtypeStruct((latents, 4 * tokens), jnp.bfloat16),
        in_specs=[SCALARS] + [ONCHIP] * 4,
        out_specs=ONCHIP,
        compiler_params=limit(8),
    )(place, *shares(packed))

    lanes = jax.ShapeDtypeStruct((latents, LANES), f32)
    slab = jax.ShapeDtypeStruct((latents, width), f32)
    kept_slab = pltpu.VMEM((latents, width), f32)
    kept_decoder = resident(decoder)
    squares = pl.pallas_call(
        squares_kernel,
        out_shape=jax.ShapeDtypeStruct((1, latents), f32),
        in_specs=[ONCHIP],
        out_specs=ONCHIP,
        scratch_shapes=[pltpu.VMEM((latents, LANES), f32)],
        compiler_params=limit(8),
    )(resident(after(decoder, near)))
    early = pl.pallas_call(
        early_kernel,
        out_shape=kept_slab,
        in_specs=[ONCHIP] + [OUTSIDE] * 8,
        out_specs=ONCHIP,
        scratch_shapes=[pltpu.VMEM((5 * tokens, width), jnp.bfloat16), pltpu.SemaphoreType.DMA((8,))],
        compiler_params=limit(10),
        cost_estimate=pl.CostEstimate(flops=20 * latents * tokens * width, bytes_accessed=16 * latents * width, transcendentals=0),
    )(codes, *map(outside, (errors, near, *end2, *mid2, *mid3)))
    gradient, sums = pl.pallas_call(
        along_kernel,
        out_shape=(kept_slab, jax.ShapeDtypeStruct((2, latents), f32)),
        in_specs=[ONCHIP] * 6,
        out_specs=(ONCHIP,) * 2,
        scratch_shapes=[pltpu.VMEM((latents, LANES), f32)],
        compiler_params=limit(8),
    )(codes, resident(end3[0]), resident(end3[1]), resident(early), kept_decoder, squares)

    scaled_first, scaled_second = pl.pallas_call(
        scale_kernel,
        out_shape=(kept_slab, kept_slab),
        in_specs=[ONCHIP] * 2,
        out_specs=(ONCHIP,) * 2,
        compiler_params=limit(4),
    )(resident(after(first_moment, mid2[0])), resident(after(second_moment, mid2[0])))
    kept_gradient = resident(gradient)
    out_sems = pltpu.SemaphoreType.DMA((latents // PART,))
    moved, ratio, lengths, new_first = pl.pallas_call(
        move_kernel,
        out_shape=(kept_slab, lanes, jax.ShapeDtypeStruct((1, latents), f32), slab),
        in_specs=[ONCHIP] * 8,
        out_specs=(ONCHIP,) * 3 + (OUTSIDE,),
        scratch_shapes=[pltpu.VMEM((latents, LANES), f32), pltpu.VMEM((latents, width), f32), out_sems],
        compiler_params=limit(8),
    )(*shares(sums), kept_gradient, kept_decoder, resident(scaled_first), resident(scaled_second))
    new_second = pl.pallas_call(
        second_kernel,
        out_shape=slab,
        in_specs=[ONCHIP] * 4,
        out_specs=OUTSIDE,
        scratch_shapes=[pltpu.VMEM((latents, width), f32), out_sems],
        compiler_params=limit(8),
        cost_estimate=pl.CostEstimate(flops=10 * latents * width, bytes_accessed=8 * latents * width, transcendentals=0),
    )(ratio, kept_gradient, kept_decoder, resident(second_moment))

    new_decoder = pl.pallas_call(
        unit_kernel,
        out_shape=slab,
        in_specs=[ONCHIP] * 5,
        out_specs=OUTSIDE,
        scratch_shapes=[pltpu.VMEM((latents, width), f32), out_sems],
        compiler_params=limit(8),
    )(*shares(lengths), resident(moved))
    return (new_decoder, new_first, new_second)


def gather_body(errors, block_ids, code_values, decoder, first_moment, second_moment):
    here = lax.axis_index("lat")
    lat_dev = decoder.shape[0]
    blk_dev = lat_dev // BLOCK
    every_ids = lax.all_gather(block_ids, "lat", axis=0, tiled=True)
    owned = here * blk_dev + jnp.arange(blk_dev, dtype=jnp.int32)
    err_piece = lax.all_gather(errors, "lat", axis=0, tiled=True)
    code_piece = lax.all_gather(code_values, "lat", axis=0, tiled=True)
    count = err_piece.shape[0]
    dense = jnp.zeros((count, blk_dev, BLOCK), jnp.bfloat16)
    for position in range(KB):
        match = every_ids[:, position][:, None] == owned[None, :]
        dense = dense + jnp.where(
            match[:, :, None], code_piece[:, position][:, None, :], jnp.zeros((), jnp.bfloat16)
        )
    dense = dense.reshape(count, blk_dev * BLOCK)
    gradient = lax.dot_general(
        dense, err_piece, (((0,), (0,)), ((), ())), preferred_element_type=jnp.float32
    )
    along, row_squares = lax.psum(
        (jnp.sum(gradient * decoder, axis=1), jnp.sum(decoder * decoder, axis=1)), "wid"
    )
    projected = gradient - (along / (row_squares + norm_epsilon))[:, None] * decoder
    new_first = beta_first * first_moment + (1.0 - beta_first) * projected
    new_second = beta_second * second_moment + (1.0 - beta_second) * projected * projected
    moved = decoder - learn_rate * (new_first / (1.0 - beta_first**ADAM_STEP)) / (
        jnp.sqrt(new_second / (1.0 - beta_second**ADAM_STEP)) + adam_epsilon
    )
    length_sq = lax.psum(jnp.sum(moved * moved, axis=1), "wid")
    new_decoder = moved / jnp.sqrt(length_sq + norm_epsilon)[:, None]
    return (new_decoder, new_first, new_second)


def solution(mesh):
    chain = mesh.shape["lat"] == 4 and mesh.shape["wid"] == 4
    in_specs = (
        P(("groups", "lat"), "wid"),
        P(("groups", "lat"), None),
        P(("groups", "lat"), None, None),
        P(("groups", "lat"), "wid"),
        P(("groups", "lat"), "wid"),
        P(("groups", "lat"), "wid"),
    )
    out_specs = (
        P(("groups", "lat"), "wid"),
        P(("groups", "lat"), "wid"),
        P(("groups", "lat"), "wid"),
    )
    body = chain_body if chain else gather_body
    return jax.shard_map(body, mesh=mesh, in_specs=in_specs, out_specs=out_specs, check_vma=False)
```

```python
import jax
import jax.numpy as jnp
from jax import lax
from jax.experimental import pallas as pl
from jax.experimental.pallas import tpu as pltpu
from jax.sharding import PartitionSpec as P

KB = 4
BLOCK = 128
ADAM_STEP = 100


beta_first = 0.9
beta_second = 0.999
learn_rate = 0.001
adam_epsilon = 1e-08
norm_epsilon = 1e-06

first_scale = 1.0 / (1.0 - beta_first**ADAM_STEP)
second_scale = 1.0 / (1.0 - beta_second**ADAM_STEP)

LANES = 128
MOST = 128
WIDE_BITS = (0, 1, 2, 3)
PAIR = ((0, 1), (1, 0), (2, 3), (3, 2))
MIDDLE = ((1, 2), (2, 1))
OUTWARD = ((1, 0), (2, 3))
f32 = jnp.float32


def after(value, *earlier):
    return lax.optimization_barrier((value,) + earlier)[0]


def swap(value, axis, size, bit):
    return lax.ppermute(value, axis, [(i, i ^ bit) for i in range(size)])


def row_of(lanes):
    return jnp.sum(lanes.T, axis=0, keepdims=True)


def column_of(row):
    return jnp.broadcast_to(row, (LANES, row.shape[1])).T


def fold(block):
    total = block[:, :LANES]
    for left in range(LANES, block.shape[1], LANES):
        total = total + block[:, left : left + LANES]
    return total


def pack_kernel(place_ref, ids_ref, codes_ref, out_ref):
    positions, tokens = ids_ref.shape
    names = [ids_ref[k : k + 1, :] for k in range(positions)]
    values = [codes_ref[k].astype(f32) for k in range(positions)]
    earlier = lax.broadcasted_iota(jnp.int32, (tokens, tokens), 0) < lax.broadcasted_iota(jnp.int32, (tokens, tokens), 1)
    earlier = earlier.astype(f32).astype(jnp.bfloat16)
    slots = lax.broadcasted_iota(jnp.int32, (MOST, tokens), 0).astype(f32)
    numbers = lax.broadcasted_iota(jnp.int32, (16, tokens), 1).astype(f32).astype(jnp.bfloat16)
    by_last = (((1,), (1,)), ((), ()))
    for owner in range(out_ref.shape[0]):
        block = owner * positions + place_ref[1]
        total = jnp.zeros((BLOCK, tokens), f32)
        named = jnp.zeros((1, tokens), f32)
        for name, value in zip(names, values):
            match = name == block
            total = total + jnp.where(match, value, 0.0)
            named = named + jnp.where(match, 1.0, 0.0)
        before = jnp.dot(
            jnp.broadcast_to(named, (8, tokens)).astype(jnp.bfloat16), earlier, preferred_element_type=f32
        )[:1]
        place = jnp.where(named > 0.0, before, -1.0)
        chosen = jnp.where(slots == place, 1.0, 0.0).astype(jnp.bfloat16)
        packed = lax.dot_general(total.astype(jnp.bfloat16), chosen, by_last, preferred_element_type=f32)
        out_ref[owner, :BLOCK, :] = packed.astype(jnp.bfloat16)
        whose = lax.dot_general(numbers, chosen, by_last, preferred_element_type=f32)
        out_ref[owner, BLOCK:, :] = whose.astype(jnp.bfloat16)


def dense_kernel(place_ref, *refs):
    *packed_refs, out_ref = refs
    count = packed_refs[0].shape[0]
    tokens = out_ref.shape[1] // count
    numbers = lax.broadcasted_iota(jnp.int32, (MOST, LANES), 1).astype(f32)
    for packed_ref, bit in zip(packed_refs, WIDE_BITS):
        block = place_ref[1] ^ bit
        rows = pl.ds(pl.multiple_of(block * BLOCK, BLOCK), BLOCK)
        for order in range(count):
            source = place_ref[0] ^ order
            whose = column_of(packed_ref[source, BLOCK:, :].astype(f32)[:1])
            for left in range(0, tokens, LANES):
                chosen = jnp.where(whose == numbers + float(left), 1.0, 0.0).astype(jnp.bfloat16)
                spread = jnp.dot(packed_ref[source, :BLOCK, :], chosen, preferred_element_type=f32)
                top = order * tokens + left
                out_ref[rows, top : top + LANES] = spread.astype(jnp.bfloat16)


def squares_kernel(decoder_ref, out_ref, lanes_ref):
    chunk = 8

    def step(index, carry):
        rows = pl.ds(pl.multiple_of(index * chunk, chunk), chunk)
        weights = decoder_ref[rows, :]
        lanes_ref[rows, :] = fold(weights * weights)
        return carry

    lax.fori_loop(0, lanes_ref.shape[0] // chunk, step, 0, unroll=2)
    out_ref[...] = row_of(lanes_ref[...])


def early_kernel(codes_ref, *refs):
    *piece_refs, grad_ref, rows_ref, sems = refs
    width = grad_ref.shape[1]
    copies, top = [], 0
    for index, piece in enumerate(piece_refs):
        high = piece.shape[0]
        copies.append(
            pltpu.make_async_copy(
                piece.at[:, pl.ds(0, width)], rows_ref.at[pl.ds(top, high)], sems.at[index]
            )
        )
        copies[-1].start()
        top += high
    for copy in copies:
        copy.wait()
    block = 512
    tokens = codes_ref.shape[1] // 4
    for left in range(0, width, block):
        columns = slice(left, left + block)
        grad_ref[:, columns] = jnp.dot(
            codes_ref[:, : 3 * tokens], rows_ref[: 3 * tokens, columns], preferred_element_type=f32
        ) + jnp.dot(codes_ref[:, 2 * tokens :], rows_ref[3 * tokens :, columns], preferred_element_type=f32)


def along_kernel(codes_ref, last0_ref, last1_ref, early_ref, decoder_ref, squares_ref, grad_ref, out_ref, total_ref):
    late_codes = codes_ref[:, codes_ref.shape[1] // 4 * 3 :]
    block = 512
    for left in range(0, grad_ref.shape[1], block):
        columns = slice(left, left + block)
        rows = jnp.concatenate([last0_ref[:, columns], last1_ref[:, columns]], axis=0)
        gradient = early_ref[:, columns] + jnp.dot(late_codes, rows, preferred_element_type=f32)
        grad_ref[:, columns] = gradient
        share = fold(gradient * decoder_ref[:, columns])
        total_ref[...] = share if left == 0 else total_ref[...] + share
    out_ref[0:1, :] = row_of(total_ref[...])
    out_ref[1:2, :] = squares_ref[...]


def ratio_of(sum0_ref, sum1_ref, sum2_ref, sum3_ref):
    sums = (sum0_ref[...] + sum1_ref[...]) + (sum2_ref[...] + sum3_ref[...])
    return column_of(sums[0:1] / (sums[1:2] + norm_epsilon))


PART = 64


def rows_out(buf, target, sems):
    parts = [pl.ds(index * PART, PART) for index in range(buf.shape[0] // PART)]
    return [pltpu.make_async_copy(buf.at[rows], target.at[rows], sems.at[i]) for i, rows in enumerate(parts)]


def scale_kernel(first_ref, second_ref, scaled_first_ref, scaled_second_ref):
    chunk = 8

    def step(index, carry):
        rows = pl.ds(pl.multiple_of(index * chunk, chunk), chunk)
        scaled_first_ref[rows, :] = beta_first * first_ref[rows, :]
        scaled_second_ref[rows, :] = (beta_second * second_scale) * second_ref[rows, :]
        return carry

    lax.fori_loop(0, first_ref.shape[0] // chunk, step, 0, unroll=2)


def move_kernel(sum0_ref, sum1_ref, sum2_ref, sum3_ref, grad_ref, decoder_ref, scaled_first_ref, scaled_second_ref,
                moved_ref, ratio_ref, out_ref, new_first_ref, total_ref, first_buf, sems):
    ratio_ref[...] = ratio_of(sum0_ref, sum1_ref, sum2_ref, sum3_ref)
    width = grad_ref.shape[1]
    chunk = 8
    copies = rows_out(first_buf, new_first_ref, sems)
    for index, copy in enumerate(copies):

        def step(inner, carry):
            rows = pl.ds(pl.multiple_of(index * PART + inner * chunk, chunk), chunk)
            ratio = ratio_ref[rows, :]
            total = jnp.zeros((chunk, LANES), f32)
            for left in range(0, width, LANES):
                columns = slice(left, left + LANES)
                weights = decoder_ref[rows, columns]
                projected = grad_ref[rows, columns] - ratio * weights
                new_first = scaled_first_ref[rows, columns] + (1.0 - beta_first) * projected
                first_buf[rows, columns] = new_first
                unbiased = scaled_second_ref[rows, columns] + ((1.0 - beta_second) * second_scale) * (projected * projected)
                spread = unbiased * lax.rsqrt(unbiased) + adam_epsilon
                moved = weights - (learn_rate * first_scale) * new_first / spread
                moved_ref[rows, columns] = moved
                total = total + moved * moved
            total_ref[rows, :] = total
            return carry

        lax.fori_loop(0, PART // chunk, step, 0, unroll=PART // chunk)
        copy.start()
    out_ref[...] = row_of(total_ref[...])
    for copy in copies:
        copy.wait()


def second_kernel(ratio_ref, grad_ref, decoder_ref, second_ref, new_second_ref, second_buf, sems):
    width = grad_ref.shape[1]
    chunk = 8
    copies = rows_out(second_buf, new_second_ref, sems)
    for index, copy in enumerate(copies):

        def step(inner, carry):
            rows = pl.ds(pl.multiple_of(index * PART + inner * chunk, chunk), chunk)
            ratio = ratio_ref[rows, :]
            for left in range(0, width, LANES):
                columns = slice(left, left + LANES)
                projected = grad_ref[rows, columns] - ratio * decoder_ref[rows, columns]
                second = second_ref[rows, columns]
                second_buf[rows, columns] = beta_second * second + ((1.0 - beta_second) * projected) * projected
            return carry

        lax.fori_loop(0, PART // chunk, step, 0, unroll=4)
        copy.start()
    for copy in copies:
        copy.wait()


def unit_kernel(sum0_ref, sum1_ref, sum2_ref, sum3_ref, moved_ref, out_ref, buf, sems):
    length = (sum0_ref[...] + sum1_ref[...]) + (sum2_ref[...] + sum3_ref[...])
    scale = column_of(1.0 / jnp.sqrt(length + norm_epsilon))
    width = moved_ref.shape[1]
    copies = rows_out(buf, out_ref, sems)
    for index, copy in enumerate(copies):
        rows = slice(index * PART, (index + 1) * PART)
        for left in range(0, width, LANES):
            buf[rows, left : left + LANES] = moved_ref[rows, left : left + LANES] * scale[rows]
        copy.start()
    for copy in copies:
        copy.wait()


SCALARS = pl.BlockSpec(memory_space=pltpu.SMEM)
ONCHIP = pl.BlockSpec(memory_space=pltpu.VMEM)
OUTSIDE = pl.BlockSpec(memory_space=pl.ANY)


def resident(value):
    return pltpu.with_memory_space_constraint(value, pltpu.VMEM)


def outside(value):
    return pltpu.with_memory_space_constraint(value, pltpu.HBM)


def limit(mib):
    return pltpu.CompilerParams(vmem_limit_bytes=mib * 1024 * 1024)


def shares(value):
    return [value] + [swap(value, "wid", 4, bit) for bit in WIDE_BITS[1:]]


def chain_body(errors, block_ids, code_values, decoder, first_moment, second_moment):
    here = lax.axis_index("lat")
    wide = lax.axis_index("wid")
    place = jnp.stack([here, wide]).astype(jnp.int32)
    tokens, width = errors.shape
    half = tokens // 2
    latents = decoder.shape[0]

    hop = lambda value, pairs: lax.ppermute(value, "lat", pairs)
    near = hop(errors, PAIR)
    packed = pl.pallas_call(
        pack_kernel,
        out_shape=jax.ShapeDtypeStruct((4, BLOCK + 16, MOST), jnp.bfloat16),
        in_specs=[SCALARS] + [ONCHIP] * 2,
        out_specs=ONCHIP,
        compiler_params=limit(8),
    )(place, block_ids.T, code_values.transpose(1, 2, 0))
    packed = lax.all_to_all(packed, "lat", 0, 0, tiled=True)

    mid3 = [hop(errors[i * half : (i + 1) * half], MIDDLE) for i in range(2)]
    end2 = [hop(part, OUTWARD) for part in mid3]
    near = after(near, mid3[0])
    mid2 = [hop(near[:half], MIDDLE), hop(after(near, mid3[1], packed)[half:], MIDDLE)]
    end3 = [hop(after(mid2[0], end2[0]), OUTWARD), hop(mid2[1], OUTWARD)]

    packed = after(packed, mid3[1])
    codes = pl.pallas_call(
        dense_kernel,
        out_shape=jax.ShapeDtypeStruct((latents, 4 * tokens), jnp.bfloat16),
        in_specs=[SCALARS] + [ONCHIP] * 4,
        out_specs=ONCHIP,
        compiler_params=limit(8),
    )(place, *shares(packed))

    lanes = jax.ShapeDtypeStruct((latents, LANES), f32)
    slab = jax.ShapeDtypeStruct((latents, width), f32)
    kept_slab = pltpu.VMEM((latents, width), f32)
    kept_decoder = resident(decoder)
    squares = pl.pallas_call(
        squares_kernel,
        out_shape=jax.ShapeDtypeStruct((1, latents), f32),
        in_specs=[ONCHIP],
        out_specs=ONCHIP,
        scratch_shapes=[pltpu.VMEM((latents, LANES), f32)],
        compiler_params=limit(8),
    )(resident(after(decoder, near)))
    early = pl.pallas_call(
        early_kernel,
        out_shape=kept_slab,
        in_specs=[ONCHIP] + [OUTSIDE] * 8,
        out_specs=ONCHIP,
        scratch_shapes=[pltpu.VMEM((5 * tokens, width), jnp.bfloat16), pltpu.SemaphoreType.DMA((8,))],
        compiler_params=limit(10),
        cost_estimate=pl.CostEstimate(flops=20 * latents * tokens * width, bytes_accessed=16 * latents * width, transcendentals=0),
    )(codes, *map(outside, (errors, near, *end2, *mid2, *mid3)))
    gradient, sums = pl.pallas_call(
        along_kernel,
        out_shape=(kept_slab, jax.ShapeDtypeStruct((2, latents), f32)),
        in_specs=[ONCHIP] * 6,
        out_specs=(ONCHIP,) * 2,
        scratch_shapes=[pltpu.VMEM((latents, LANES), f32)],
        compiler_params=limit(8),
    )(codes, resident(end3[0]), resident(end3[1]), resident(early), kept_decoder, squares)

    scaled_first, scaled_second = pl.pallas_call(
        scale_kernel,
        out_shape=(kept_slab, kept_slab),
        in_specs=[ONCHIP] * 2,
        out_specs=(ONCHIP,) * 2,
        compiler_params=limit(4),
    )(resident(after(first_moment, mid2[0])), resident(after(second_moment, mid2[0])))
    kept_gradient = resident(gradient)
    out_sems = pltpu.SemaphoreType.DMA((latents // PART,))
    moved, ratio, lengths, new_first = pl.pallas_call(
        move_kernel,
        out_shape=(kept_slab, lanes, jax.ShapeDtypeStruct((1, latents), f32), slab),
        in_specs=[ONCHIP] * 8,
        out_specs=(ONCHIP,) * 3 + (OUTSIDE,),
        scratch_shapes=[pltpu.VMEM((latents, LANES), f32), pltpu.VMEM((latents, width), f32), out_sems],
        compiler_params=limit(8),
    )(*shares(sums), kept_gradient, kept_decoder, resident(scaled_first), resident(scaled_second))
    new_second = pl.pallas_call(
        second_kernel,
        out_shape=slab,
        in_specs=[ONCHIP] * 4,
        out_specs=OUTSIDE,
        scratch_shapes=[pltpu.VMEM((latents, width), f32), out_sems],
        compiler_params=limit(8),
        cost_estimate=pl.CostEstimate(flops=10 * latents * width, bytes_accessed=8 * latents * width, transcendentals=0),
    )(ratio, kept_gradient, kept_decoder, resident(second_moment))

    new_decoder = pl.pallas_call(
        unit_kernel,
        out_shape=slab,
        in_specs=[ONCHIP] * 5,
        out_specs=OUTSIDE,
        scratch_shapes=[pltpu.VMEM((latents, width), f32), out_sems],
        compiler_params=limit(8),
    )(*shares(lengths), resident(moved))
    return (new_decoder, new_first, new_second)


def gather_body(errors, block_ids, code_values, decoder, first_moment, second_moment):
    here = lax.axis_index("lat")
    lat_dev = decoder.shape[0]
    blk_dev = lat_dev // BLOCK
    every_ids = lax.all_gather(block_ids, "lat", axis=0, tiled=True)
    owned = here * blk_dev + jnp.arange(blk_dev, dtype=jnp.int32)
    err_piece = lax.all_gather(errors, "lat", axis=0, tiled=True)
    code_piece = lax.all_gather(code_values, "lat", axis=0, tiled=True)
    count = err_piece.shape[0]
    dense = jnp.zeros((count, blk_dev, BLOCK), jnp.bfloat16)
    for position in range(KB):
        match = every_ids[:, position][:, None] == owned[None, :]
        dense = dense + jnp.where(
            match[:, :, None], code_piece[:, position][:, None, :], jnp.zeros((), jnp.bfloat16)
        )
    dense = dense.reshape(count, blk_dev * BLOCK)
    gradient = lax.dot_general(
        dense, err_piece, (((0,), (0,)), ((), ())), preferred_element_type=jnp.float32
    )
    along, row_squares = lax.psum(
        (jnp.sum(gradient * decoder, axis=1), jnp.sum(decoder * decoder, axis=1)), "wid"
    )
    projected = gradient - (along / (row_squares + norm_epsilon))[:, None] * decoder
    new_first = beta_first * first_moment + (1.0 - beta_first) * projected
    new_second = beta_second * second_moment + (1.0 - beta_second) * projected * projected
    moved = decoder - learn_rate * (new_first / (1.0 - beta_first**ADAM_STEP)) / (
        jnp.sqrt(new_second / (1.0 - beta_second**ADAM_STEP)) + adam_epsilon
    )
    length_sq = lax.psum(jnp.sum(moved * moved, axis=1), "wid")
    new_decoder = moved / jnp.sqrt(length_sq + norm_epsilon)[:, None]
    return (new_decoder, new_first, new_second)


def solution(mesh):
    chain = mesh.shape["lat"] == 4 and mesh.shape["wid"] == 4
    in_specs = (
        P(("groups", "lat"), "wid"),
        P(("groups", "lat"), None),
        P(("groups", "lat"), None, None),
        P(("groups", "lat"), "wid"),
        P(("groups", "lat"), "wid"),
        P(("groups", "lat"), "wid"),
    )
    out_specs = (
        P(("groups", "lat"), "wid"),
        P(("groups", "lat"), "wid"),
        P(("groups", "lat"), "wid"),
    )
    body = chain_body if chain else gather_body
    return jax.shard_map(body, mesh=mesh, in_specs=in_specs, out_specs=out_specs, check_vma=False)
```

```python
import jax
import jax.numpy as jnp
from jax import lax
from jax.experimental import pallas as pl
from jax.experimental.pallas import tpu as pltpu
from jax.sharding import PartitionSpec as P

KB = 4
BLOCK = 128
ADAM_STEP = 100


beta_first = 0.9
beta_second = 0.999
learn_rate = 0.001
adam_epsilon = 1e-08
norm_epsilon = 1e-06

first_scale = 1.0 / (1.0 - beta_first**ADAM_STEP)
second_scale = 1.0 / (1.0 - beta_second**ADAM_STEP)

LANES = 128
MOST = 128
WIDE_BITS = (0, 1, 2, 3)
PAIR = ((0, 1), (1, 0), (2, 3), (3, 2))
MIDDLE = ((1, 2), (2, 1))
OUTWARD = ((1, 0), (2, 3))
f32 = jnp.float32


def after(value, *earlier):
    return lax.optimization_barrier((value,) + earlier)[0]


def swap(value, axis, size, bit):
    return lax.ppermute(value, axis, [(i, i ^ bit) for i in range(size)])


def row_of(lanes):
    return jnp.sum(lanes.T, axis=0, keepdims=True)


def column_of(row):
    return jnp.broadcast_to(row, (LANES, row.shape[1])).T


def fold(block):
    total = block[:, :LANES]
    for left in range(LANES, block.shape[1], LANES):
        total = total + block[:, left : left + LANES]
    return total


def pack_kernel(place_ref, ids_ref, codes_ref, out_ref):
    positions, tokens = ids_ref.shape
    names = [ids_ref[k : k + 1, :] for k in range(positions)]
    values = [codes_ref[k].astype(f32) for k in range(positions)]
    earlier = lax.broadcasted_iota(jnp.int32, (tokens, tokens), 0) < lax.broadcasted_iota(jnp.int32, (tokens, tokens), 1)
    earlier = earlier.astype(f32).astype(jnp.bfloat16)
    slots = lax.broadcasted_iota(jnp.int32, (MOST, tokens), 0).astype(f32)
    numbers = lax.broadcasted_iota(jnp.int32, (16, tokens), 1).astype(f32).astype(jnp.bfloat16)
    by_last = (((1,), (1,)), ((), ()))
    for owner in range(out_ref.shape[0]):
        block = owner * positions + place_ref[1]
        total = jnp.zeros((BLOCK, tokens), f32)
        named = jnp.zeros((1, tokens), f32)
        for name, value in zip(names, values):
            match = name == block
            total = total + jnp.where(match, value, 0.0)
            named = named + jnp.where(match, 1.0, 0.0)
        before = jnp.dot(
            jnp.broadcast_to(named, (8, tokens)).astype(jnp.bfloat16), earlier, preferred_element_type=f32
        )[:1]
        place = jnp.where(named > 0.0, before, -1.0)
        chosen = jnp.where(slots == place, 1.0, 0.0).astype(jnp.bfloat16)
        packed = lax.dot_general(total.astype(jnp.bfloat16), chosen, by_last, preferred_element_type=f32)
        out_ref[owner, :BLOCK, :] = packed.astype(jnp.bfloat16)
        whose = lax.dot_general(numbers, chosen, by_last, preferred_element_type=f32)
        out_ref[owner, BLOCK:, :] = whose.astype(jnp.bfloat16)


def dense_kernel(place_ref, *refs):
    *packed_refs, out_ref = refs
    count = packed_refs[0].shape[0]
    tokens = out_ref.shape[1] // count
    numbers = lax.broadcasted_iota(jnp.int32, (MOST, LANES), 1).astype(f32)
    for packed_ref, bit in zip(packed_refs, WIDE_BITS):
        block = place_ref[1] ^ bit
        rows = pl.ds(pl.multiple_of(block * BLOCK, BLOCK), BLOCK)
        for order in range(count):
            source = place_ref[0] ^ order
            whose = column_of(packed_ref[source, BLOCK:, :].astype(f32)[:1])
            for left in range(0, tokens, LANES):
                chosen = jnp.where(whose == numbers + float(left), 1.0, 0.0).astype(jnp.bfloat16)
                spread = jnp.dot(packed_ref[source, :BLOCK, :], chosen, preferred_element_type=f32)
                top = order * tokens + left
                out_ref[rows, top : top + LANES] = spread.astype(jnp.bfloat16)


def squares_kernel(decoder_ref, out_ref, lanes_ref):
    chunk = 8

    def step(index, carry):
        rows = pl.ds(pl.multiple_of(index * chunk, chunk), chunk)
        weights = decoder_ref[rows, :]
        lanes_ref[rows, :] = fold(weights * weights)
        return carry

    lax.fori_loop(0, lanes_ref.shape[0] // chunk, step, 0, unroll=2)
    out_ref[...] = row_of(lanes_ref[...])


def early_kernel(codes_ref, *refs):
    *piece_refs, grad_ref, rows_ref, sems = refs
    width = grad_ref.shape[1]
    copies, top = [], 0
    for index, piece in enumerate(piece_refs):
        high = piece.shape[0]
        copies.append(
            pltpu.make_async_copy(
                piece.at[:, pl.ds(0, width)], rows_ref.at[pl.ds(top, high)], sems.at[index]
            )
        )
        copies[-1].start()
        top += high
    for copy in copies:
        copy.wait()
    block = 512
    tokens = codes_ref.shape[1] // 4
    for left in range(0, width, block):
        columns = slice(left, left + block)
        grad_ref[:, columns] = jnp.dot(
            codes_ref[:, : 3 * tokens], rows_ref[: 3 * tokens, columns], preferred_element_type=f32
        ) + jnp.dot(codes_ref[:, 2 * tokens :], rows_ref[3 * tokens :, columns], preferred_element_type=f32)


def along_kernel(codes_ref, last0_ref, last1_ref, early_ref, decoder_ref, squares_ref, grad_ref, out_ref, total_ref):
    late_codes = codes_ref[:, codes_ref.shape[1] // 4 * 3 :]
    block = 512
    for left in range(0, grad_ref.shape[1], block):
        columns = slice(left, left + block)
        rows = jnp.concatenate([last0_ref[:, columns], last1_ref[:, columns]], axis=0)
        gradient = early_ref[:, columns] + jnp.dot(late_codes, rows, preferred_element_type=f32)
        grad_ref[:, columns] = gradient
        share = fold(gradient * decoder_ref[:, columns])
        total_ref[...] = share if left == 0 else total_ref[...] + share
    out_ref[0:1, :] = row_of(total_ref[...])
    out_ref[1:2, :] = squares_ref[...]


def ratio_of(sum0_ref, sum1_ref, sum2_ref, sum3_ref):
    sums = (sum0_ref[...] + sum1_ref[...]) + (sum2_ref[...] + sum3_ref[...])
    return column_of(sums[0:1] / (sums[1:2] + norm_epsilon))


PART = 64


def rows_out(buf, target, sems):
    parts = [pl.ds(index * PART, PART) for index in range(buf.shape[0] // PART)]
    return [pltpu.make_async_copy(buf.at[rows], target.at[rows], sems.at[i]) for i, rows in enumerate(parts)]


def scale_kernel(first_ref, second_ref, scaled_first_ref, scaled_second_ref):
    chunk = 8

    def step(index, carry):
        rows = pl.ds(pl.multiple_of(index * chunk, chunk), chunk)
        scaled_first_ref[rows, :] = beta_first * first_ref[rows, :]
        scaled_second_ref[rows, :] = (beta_second * second_scale) * second_ref[rows, :]
        return carry

    lax.fori_loop(0, first_ref.shape[0] // chunk, step, 0, unroll=2)


def move_kernel(sum0_ref, sum1_ref, sum2_ref, sum3_ref, grad_ref, decoder_ref, scaled_first_ref, scaled_second_ref,
                moved_ref, ratio_ref, out_ref, new_first_ref, total_ref, first_buf, sems):
    ratio_ref[...] = ratio_of(sum0_ref, sum1_ref, sum2_ref, sum3_ref)
    width = grad_ref.shape[1]
    chunk = 8
    copies = rows_out(first_buf, new_first_ref, sems)
    for index, copy in enumerate(copies):

        def step(inner, carry):
            rows = pl.ds(pl.multiple_of(index * PART + inner * chunk, chunk), chunk)
            ratio = ratio_ref[rows, :]
            total = jnp.zeros((chunk, LANES), f32)
            for left in range(0, width, LANES):
                columns = slice(left, left + LANES)
                weights = decoder_ref[rows, columns]
                projected = grad_ref[rows, columns] - ratio * weights
                new_first = scaled_first_ref[rows, columns] + (1.0 - beta_first) * projected
                first_buf[rows, columns] = new_first
                unbiased = scaled_second_ref[rows, columns] + ((1.0 - beta_second) * second_scale) * (projected * projected)
                spread = unbiased * lax.rsqrt(unbiased) + adam_epsilon
                moved = weights - (learn_rate * first_scale) * new_first / spread
                moved_ref[rows, columns] = moved
                total = total + moved * moved
            total_ref[rows, :] = total
            return carry

        lax.fori_loop(0, PART // chunk, step, 0, unroll=PART // chunk)
        copy.start()
    out_ref[...] = row_of(total_ref[...])
    for copy in copies:
        copy.wait()


def second_kernel(ratio_ref, grad_ref, decoder_ref, second_ref, new_second_ref, second_buf, sems):
    width = grad_ref.shape[1]
    chunk = 8
    copies = rows_out(second_buf, new_second_ref, sems)
    for index, copy in enumerate(copies):

        def step(inner, carry):
            rows = pl.ds(pl.multiple_of(index * PART + inner * chunk, chunk), chunk)
            ratio = ratio_ref[rows, :]
            for left in range(0, width, LANES):
                columns = slice(left, left + LANES)
                projected = grad_ref[rows, columns] - ratio * decoder_ref[rows, columns]
                second = second_ref[rows, columns]
                second_buf[rows, columns] = beta_second * second + ((1.0 - beta_second) * projected) * projected
            return carry

        lax.fori_loop(0, PART // chunk, step, 0, unroll=4)
        copy.start()
    for copy in copies:
        copy.wait()


def unit_kernel(sum0_ref, sum1_ref, sum2_ref, sum3_ref, moved_ref, out_ref, buf, sems):
    length = (sum0_ref[...] + sum1_ref[...]) + (sum2_ref[...] + sum3_ref[...])
    scale = column_of(1.0 / jnp.sqrt(length + norm_epsilon))
    width = moved_ref.shape[1]
    copies = rows_out(buf, out_ref, sems)
    for index, copy in enumerate(copies):
        rows = slice(index * PART, (index + 1) * PART)
        for left in range(0, width, LANES):
            buf[rows, left : left + LANES] = moved_ref[rows, left : left + LANES] * scale[rows]
        copy.start()
    for copy in copies:
        copy.wait()


SCALARS = pl.BlockSpec(memory_space=pltpu.SMEM)
ONCHIP = pl.BlockSpec(memory_space=pltpu.VMEM)
OUTSIDE = pl.BlockSpec(memory_space=pl.ANY)


def resident(value):
    return pltpu.with_memory_space_constraint(value, pltpu.VMEM)


def outside(value):
    return pltpu.with_memory_space_constraint(value, pltpu.HBM)


def limit(mib):
    return pltpu.CompilerParams(vmem_limit_bytes=mib * 1024 * 1024)


def shares(value, bits=(1, 2, 3)):
    return [value] + [swap(value, "wid", 4, bit) for bit in bits]


def chain_body(errors, block_ids, code_values, decoder, first_moment, second_moment):
    here = lax.axis_index("lat")
    wide = lax.axis_index("wid")
    place = jnp.stack([here, wide]).astype(jnp.int32)
    tokens, width = errors.shape
    half = tokens // 2
    latents = decoder.shape[0]

    hop = lambda value, pairs: lax.ppermute(value, "lat", pairs)
    near = hop(errors, PAIR)
    packed = pl.pallas_call(
        pack_kernel,
        out_shape=jax.ShapeDtypeStruct((4, BLOCK + 16, MOST), jnp.bfloat16),
        in_specs=[SCALARS] + [ONCHIP] * 2,
        out_specs=ONCHIP,
        compiler_params=limit(8),
    )(place, block_ids.T, code_values.transpose(1, 2, 0))
    packed = lax.all_to_all(packed, "lat", 0, 0, tiled=True)

    mid3 = [hop(errors[i * half : (i + 1) * half], MIDDLE) for i in range(2)]
    end2 = [hop(part, OUTWARD) for part in mid3]
    near = after(near, mid3[0])
    mid2 = [hop(near[:half], MIDDLE), hop(after(near, mid3[1], packed)[half:], MIDDLE)]
    end3 = [hop(after(mid2[0], end2[0]), OUTWARD), hop(mid2[1], OUTWARD)]

    packed = after(packed, mid3[1])
    codes = pl.pallas_call(
        dense_kernel,
        out_shape=jax.ShapeDtypeStruct((latents, 4 * tokens), jnp.bfloat16),
        in_specs=[SCALARS] + [ONCHIP] * 4,
        out_specs=ONCHIP,
        compiler_params=limit(8),
    )(place, *shares(packed))

    lanes = jax.ShapeDtypeStruct((latents, LANES), f32)
    slab = jax.ShapeDtypeStruct((latents, width), f32)
    kept_slab = pltpu.VMEM((latents, width), f32)
    kept_decoder = resident(decoder)
    squares = pl.pallas_call(
        squares_kernel,
        out_shape=jax.ShapeDtypeStruct((1, latents), f32),
        in_specs=[ONCHIP],
        out_specs=ONCHIP,
        scratch_shapes=[pltpu.VMEM((latents, LANES), f32)],
        compiler_params=limit(8),
    )(resident(after(decoder, near)))
    early = pl.pallas_call(
        early_kernel,
        out_shape=kept_slab,
        in_specs=[ONCHIP] + [OUTSIDE] * 8,
        out_specs=ONCHIP,
        scratch_shapes=[pltpu.VMEM((5 * tokens, width), jnp.bfloat16), pltpu.SemaphoreType.DMA((8,))],
        compiler_params=limit(10),
        cost_estimate=pl.CostEstimate(flops=20 * latents * tokens * width, bytes_accessed=16 * latents * width, transcendentals=0),
    )(codes, *map(outside, (errors, near, *end2, *mid2, *mid3)))
    gradient, sums = pl.pallas_call(
        along_kernel,
        out_shape=(kept_slab, jax.ShapeDtypeStruct((2, latents), f32)),
        in_specs=[ONCHIP] * 6,
        out_specs=(ONCHIP,) * 2,
        scratch_shapes=[pltpu.VMEM((latents, LANES), f32)],
        compiler_params=limit(8),
    )(codes, resident(end3[0]), resident(end3[1]), resident(early), kept_decoder, squares)

    scaled_first, scaled_second = pl.pallas_call(
        scale_kernel,
        out_shape=(kept_slab, kept_slab),
        in_specs=[ONCHIP] * 2,
        out_specs=(ONCHIP,) * 2,
        compiler_params=limit(4),
    )(resident(after(first_moment, mid2[0])), resident(after(second_moment, mid2[0])))
    kept_gradient = resident(gradient)
    out_sems = pltpu.SemaphoreType.DMA((latents // PART,))
    moved, ratio, lengths, new_first = pl.pallas_call(
        move_kernel,
        out_shape=(kept_slab, lanes, jax.ShapeDtypeStruct((1, latents), f32), slab),
        in_specs=[ONCHIP] * 8,
        out_specs=(ONCHIP,) * 3 + (OUTSIDE,),
        scratch_shapes=[pltpu.VMEM((latents, LANES), f32), pltpu.VMEM((latents, width), f32), out_sems],
        compiler_params=limit(8),
    )(*shares(sums), kept_gradient, kept_decoder, resident(scaled_first), resident(scaled_second))
    new_second = pl.pallas_call(
        second_kernel,
        out_shape=slab,
        in_specs=[ONCHIP] * 4,
        out_specs=OUTSIDE,
        scratch_shapes=[pltpu.VMEM((latents, width), f32), out_sems],
        compiler_params=limit(8),
        cost_estimate=pl.CostEstimate(flops=10 * latents * width, bytes_accessed=8 * latents * width, transcendentals=0),
    )(ratio, kept_gradient, kept_decoder, resident(second_moment))

    new_decoder = pl.pallas_call(
        unit_kernel,
        out_shape=slab,
        in_specs=[ONCHIP] * 5,
        out_specs=OUTSIDE,
        scratch_shapes=[pltpu.VMEM((latents, width), f32), out_sems],
        compiler_params=limit(8),
    )(*shares(lengths, (3, 2, 1)), resident(moved))
    return (new_decoder, new_first, new_second)


def gather_body(errors, block_ids, code_values, decoder, first_moment, second_moment):
    here = lax.axis_index("lat")
    lat_dev = decoder.shape[0]
    blk_dev = lat_dev // BLOCK
    every_ids = lax.all_gather(block_ids, "lat", axis=0, tiled=True)
    owned = here * blk_dev + jnp.arange(blk_dev, dtype=jnp.int32)
    err_piece = lax.all_gather(errors, "lat", axis=0, tiled=True)
    code_piece = lax.all_gather(code_values, "lat", axis=0, tiled=True)
    count = err_piece.shape[0]
    dense = jnp.zeros((count, blk_dev, BLOCK), jnp.bfloat16)
    for position in range(KB):
        match = every_ids[:, position][:, None] == owned[None, :]
        dense = dense + jnp.where(
            match[:, :, None], code_piece[:, position][:, None, :], jnp.zeros((), jnp.bfloat16)
        )
    dense = dense.reshape(count, blk_dev * BLOCK)
    gradient = lax.dot_general(
        dense, err_piece, (((0,), (0,)), ((), ())), preferred_element_type=jnp.float32
    )
    along, row_squares = lax.psum(
        (jnp.sum(gradient * decoder, axis=1), jnp.sum(decoder * decoder, axis=1)), "wid"
    )
    projected = gradient - (along / (row_squares + norm_epsilon))[:, None] * decoder
    new_first = beta_first * first_moment + (1.0 - beta_first) * projected
    new_second = beta_second * second_moment + (1.0 - beta_second) * projected * projected
    moved = decoder - learn_rate * (new_first / (1.0 - beta_first**ADAM_STEP)) / (
        jnp.sqrt(new_second / (1.0 - beta_second**ADAM_STEP)) + adam_epsilon
    )
    length_sq = lax.psum(jnp.sum(moved * moved, axis=1), "wid")
    new_decoder = moved / jnp.sqrt(length_sq + norm_epsilon)[:, None]
    return (new_decoder, new_first, new_second)


def solution(mesh):
    chain = mesh.shape["lat"] == 4 and mesh.shape["wid"] == 4
    in_specs = (
        P(("groups", "lat"), "wid"),
        P(("groups", "lat"), None),
        P(("groups", "lat"), None, None),
        P(("groups", "lat"), "wid"),
        P(("groups", "lat"), "wid"),
        P(("groups", "lat"), "wid"),
    )
    out_specs = (
        P(("groups", "lat"), "wid"),
        P(("groups", "lat"), "wid"),
        P(("groups", "lat"), "wid"),
    )
    body = chain_body if chain else gather_body
    return jax.shard_map(body, mesh=mesh, in_specs=in_specs, out_specs=out_specs, check_vma=False)
```
